128 devices in a mesh: comp: 2 (over core), tile: 64 (over x, y, z).
Axes of the slice: x: 4, y: 4, z: 4, core: 2. Of those that a mesh axis runs over, the one named last changes fastest.
Arguments:
- tracer: float32 [2, 16, 4, 256, 1024], P('comp', None, None, 'tile'), may hold values from -6 to 6
- velocity: float32 [2, 2, 4, 256, 1024], P('comp', None, None, 'tile'), may hold values from -0.3 to 0.3
- coupling: float32 [2, 16, 256, 1024], P('comp', None, 'tile'), may hold values from 0.05 to 0.5
- sea_mask: int32 [2, 256, 1024], P('comp', 'tile'), may hold values 0 or 1
- send_rows: int32 [2, 64, 4, 2048], P('comp', 'tile'), may hold values from 0 to 3
- send_cols: int32 [2, 64, 4, 2048], P('comp', 'tile'), may hold values from 0 to 1023
- intersection_near: int32 [2, 8, 256, 1024], P('comp', None, 'tile'), may hold values from 0 to 3
- intersection_slot: int32 [2, 8, 256, 1024], P('comp', None, 'tile'), may hold values from 0 to 2047
- intersection_weight: float32 [2, 8, 256, 1024], P('comp', None, 'tile'), as said below
Outputs:
- tracer_out: float32 [2, 16, 4, 256, 1024], P('comp', None, None, 'tile')
The draws below stay inside these ranges and needn't reach their ends.
Inputs may be any that keep to these rules, and one draw needn't show every extreme that they name: `intersection_weight`: positive, summing to one over the 8 intersections of a cell.
All inputs are finite; a program needn't handle non-finite values. No bound on the sum of `sea_mask` on one device may be relied on, other than what follows from the above.
Results may differ from the reference program's by a relative error of at most 0.000088.
Values sent between devices are 32-bit elements; how exact they have to be, the bound alone decides.
No kernel may reach another device: no remote copies, remote signals or barrier semaphores. Data moves between devices by JAX's collectives and lax.ppermute only.
A program may use at most 64 MiB of HBM per device.

```python
import math
import jax
import jax.numpy as jnp
from jax import lax

CX = 4
NY = 1024
TRC = 16
LEV = 4
K = 8
NB = 4
CAP = 2048
NX = 256
N_TILE = 64


def draw_intersection_weight(key, part):
    raw = jax.random.uniform(key, (2, K, NX, NY), jnp.float32, 0.2, 1.0)
    return raw / jnp.sum(raw, axis=1, keepdims=True)


def with_ends(array, stream_key, low, high):
    extent = array.shape
    index_at = [jax.random.randint(jax.random.fold_in(stream_key, axis), (), 0, extent[axis]) for axis in range(len(extent))]
    array = array.at[tuple(index_at)].set(low)
    longest = extent.index(max(extent))
    index_at[longest] = (index_at[longest] + 1) % extent[longest]
    return array.at[tuple(index_at)].set(high)


def level_of(key, shape, cuts, least, top_value):
    def one(axis_at, parts):
        draws = jax.random.uniform(jax.random.fold_in(jax.random.fold_in(key, 6), axis_at), (parts,), jnp.float32, least / len(cuts), top_value / len(cuts))
        return jnp.repeat(jnp.exp(draws), shape[axis_at] // parts).reshape((-1,) + (1,) * (len(shape) - axis_at - 1))

    gain = one(*cuts[0])
    for cut in cuts[1:]:
        gain = gain * one(*cut)
    return gain


def noise(rng, extent, scale, bound, shards=(), dtype=jnp.bfloat16):
    array = jax.random.normal(rng, extent, jnp.float32) * scale
    if len(shards) > 0:
        array = level_of(rng, extent, shards, -0.22, 0.18) * array
    return jnp.clip(array, min=-bound, max=bound).astype(dtype)


def setup_inputs(seed: int = 0) -> dict:
    splits = jax.random.split(jax.random.key(seed), 10)
    return {
        "tracer": noise(splits[0], (2, TRC, LEV, NX, NY), 1.0, 6.0, ((0, 2), (3, 64)), jnp.float32),
        "velocity": jnp.clip(jax.random.uniform(splits[1], (2, 2, LEV, NX, NY), jnp.float32, -0.3, 0.3) * level_of(splits[1], (2, 2, LEV, NX, NY), ((0, 2), (3, 64)), -0.4, 0.0), -0.3, 0.3),
        "coupling": jnp.clip(jnp.exp(math.log(0.5) - 2.3025851 * jax.random.uniform(splits[2], (2, TRC, NX, NY), jnp.float32) ** level_of(splits[2], (2, TRC, NX, NY), ((0, 2), (2, 64)), -0.2, 0.2)), 0.05, 0.5),
        "sea_mask": with_ends((jax.random.randint(splits[3], (2, NX, NY), 0, 4) < 3).astype(jnp.int32), jax.random.fold_in(splits[3], 1), 0, 1),
        "send_rows": with_ends(jax.random.randint(splits[4], (2, N_TILE, NB, CAP), 0, CX), jax.random.fold_in(splits[4], 1), 0, CX - 1).astype(jnp.int32),
        "send_cols": with_ends(jax.random.randint(splits[5], (2, N_TILE, NB, CAP), 0, NY), jax.random.fold_in(splits[5], 1), 0, NY - 1).astype(jnp.int32),
        "intersection_near": with_ends(jax.random.randint(splits[6], (2, K, NX, NY), 0, NB), jax.random.fold_in(splits[6], 1), 0, NB - 1).astype(jnp.int32),
        "intersection_slot": with_ends(jax.random.randint(splits[7], (2, K, NX, NY), 0, CAP), jax.random.fold_in(splits[7], 1), 0, CAP - 1).astype(jnp.int32),
        "intersection_weight": draw_intersection_weight(jax.random.fold_in(splits[9], 71), 0),
    }


diffusion = 0.12


def substep(field, speed):
    east = jnp.roll(field, -1, axis=2)
    west = jnp.roll(field, 1, axis=2)
    north = jnp.roll(field, -1, axis=3)
    south = jnp.roll(field, 1, axis=3)
    return field - 0.5 * speed[0] * (east - west) - 0.5 * speed[1] * (north - south) + diffusion * (east + west + north + south - 4.0 * field)


def reference(tracer, velocity, coupling, sea_mask, send_rows, send_cols, intersection_near, intersection_slot, intersection_weight):
    results = []
    for comp in range(2):
        other = 1 - comp
        surface = tracer[other, :, 0].reshape(TRC, NX * NY)
        xpos = lax.broadcasted_iota(jnp.int32, (NX, NY), 0)
        dest_tile = xpos // CX
        remapped = jnp.zeros((TRC, NX, NY), jnp.float32)
        for k in range(K):
            near = intersection_near[comp, k]
            source = ((dest_tile + near - 1 + N_TILE) % N_TILE).astype(jnp.int32)
            within = intersection_slot[comp, k]
            row_local = send_rows[other][source, near, within]
            col_local = send_cols[other][source, near, within]
            cell = ((source * CX + row_local) * NY + col_local).astype(jnp.int32)
            picked = jnp.take(surface, cell.reshape(-1), axis=1).reshape(TRC, NX, NY)
            remapped = remapped + intersection_weight[comp, k] * picked
        level0 = tracer[comp, :, 0]
        masked = sea_mask[comp].astype(jnp.float32)
        new0 = level0 + coupling[comp] * masked * (remapped - level0)
        field = tracer[comp].at[:, 0].set(new0)
        speed = velocity[comp]
        for step in range(2):
            field = substep(field, speed)
        results.append(field)
    return jnp.stack(results)
```

```python
import functools

import jax
import jax.numpy as jnp
from jax import lax
from jax.experimental import pallas as pl
from jax.experimental.pallas import tpu as pltpu
from jax.sharding import PartitionSpec as P

diffusion = 0.12
LOW = 128
VMEM_LIMIT = 48 * 2**20


def moved(value, steps, swap):
    tiles = lax.axis_size("tile")
    pairs = []
    for comp in range(lax.axis_size("comp")):
        for tile in range(tiles):
            target = (comp ^ 1 if swap else comp) * tiles + (tile + steps) % tiles
            pairs.append((comp * tiles + tile, target))
    return lax.ppermute(value, ("comp", "tile"), pairs)


def put_table(table, source, first, count):
    tracers = source.shape[0]
    for high in range(count):
        value = source[:, high * LOW : (high + 1) * LOW]
        leading = value.astype(jnp.bfloat16)
        rest = (value - leading.astype(jnp.float32)).astype(jnp.bfloat16)
        row = (first + high) * tracers
        table[row : row + tracers, :] = jnp.concatenate([leading, rest], axis=1)


def one_hot(low):
    width = low.shape[1]
    position = lax.broadcasted_iota(jnp.int32, (LOW, width), 0).astype(jnp.float32).astype(jnp.bfloat16)
    wanted = jnp.broadcast_to(low.astype(jnp.float32), (16, width)).astype(jnp.bfloat16)
    wanted = jnp.concatenate([wanted] * (LOW // 16), axis=0)
    return jnp.where(position == wanted, jnp.bfloat16(1), jnp.bfloat16(0))


def chosen(values, high):
    bit = 0
    while len(values) > 1:
        odd = ((high >> bit) & 1) == 1
        values = [jnp.where(odd, values[i + 1], values[i]) for i in range(0, len(values), 2)]
        bit += 1
    return values[0]


def looked_up(table, entry, tracers):
    width = entry.shape[1]
    highs = table.shape[0] // tracers
    hot = one_hot(entry & (LOW - 1))
    hot = jnp.concatenate([hot, hot], axis=0)
    product = jnp.dot(table[...], hot, preferred_element_type=jnp.float32)
    high = jnp.broadcast_to(entry // LOW, (tracers, width))
    return chosen([product[tracers * h : tracers * (h + 1)] for h in range(highs)], high)


def pack_kernel(surface, rows, cols, *rest):
    outs, table = rest[:-1], rest[-1]
    tracers, cells = surface.shape
    capacity = rows.shape[1]
    width = cells // 4
    put_table(table, surface, 0, cells // LOW)
    block = 512

    for near, out in enumerate(outs):

        def body(step, carry, near=near, out=out):
            at = pl.ds(pl.multiple_of(step * block, block), block)
            entry = rows[near : near + 1, at] * width + cols[near : near + 1, at]
            out[:, at] = looked_up(table, entry, tracers)
            return carry

        lax.fori_loop(0, capacity // block, body, 0)


def pack(surface, rows, cols):
    tracers, cells = surface.shape
    neighbours, capacity = rows.shape
    return pl.pallas_call(
        pack_kernel,
        out_shape=[jax.ShapeDtypeStruct((tracers, capacity), jnp.float32)] * neighbours,
        scratch_shapes=[pltpu.VMEM((cells // LOW * tracers, 2 * LOW), jnp.bfloat16)],
        compiler_params=pltpu.CompilerParams(vmem_limit_bytes=VMEM_LIMIT),
        cost_estimate=pl.CostEstimate(flops=4 * 10**9, bytes_accessed=10**6, transcendentals=0),
        name="pack",
    )(surface, rows, cols)


def remap_kernel(grid_rows, near, slot, weight, level0, coupling, mask, *rest):
    pieces, out, table = rest[:-2], rest[-2], rest[-1]
    tracers, capacity = pieces[0].shape
    width = level0.shape[2]
    for index, piece in enumerate(pieces):
        put_table(table, piece, index * (capacity // LOW), capacity // LOW)
    block = 512
    for place, row in enumerate(grid_rows):

        def body(step, carry, place=place, row=row):
            at = pl.ds(pl.multiple_of(step * block, block), block)
            total = jnp.zeros((tracers, block), jnp.float32)
            for k in range(near.shape[0]):
                entry = near[k, row : row + 1, at] * capacity + slot[k, row : row + 1, at]
                total = total + weight[k, row : row + 1, at] * looked_up(table, entry, tracers)
            own = level0[:, row, at]
            wet = mask[row : row + 1, at].astype(jnp.float32)
            out[:, place, at] = own + coupling[:, row, at] * wet * (total - own)
            return carry

        lax.fori_loop(0, width // block, body, 0)


def remap(grid_rows, pieces, near, slot, weight, level0, coupling, mask):
    tracers, capacity = pieces[0].shape
    return pl.pallas_call(
        functools.partial(remap_kernel, grid_rows),
        out_shape=jax.ShapeDtypeStruct((tracers, len(grid_rows), level0.shape[2]), jnp.float32),
        scratch_shapes=[pltpu.VMEM((len(pieces) * capacity // LOW * tracers, 2 * LOW), jnp.bfloat16)],
        compiler_params=pltpu.CompilerParams(vmem_limit_bytes=VMEM_LIMIT),
        cost_estimate=pl.CostEstimate(flops=15 * 10**9, bytes_accessed=10**6, transcendentals=0),
        name="remap",
    )(near, slot, weight, level0, coupling, mask, *pieces)


def substep(field, speed_x, speed_y):
    east = jnp.roll(field, -1, axis=0)
    west = jnp.roll(field, 1, axis=0)
    north = jnp.roll(field, -1, axis=1)
    south = jnp.roll(field, 1, axis=1)
    return (
        field
        - 0.5 * speed_x * (east - west)
        - 0.5 * speed_y * (north - south)
        + diffusion * (east + west + north + south - 4.0 * field)
    )


def upper_kernel(field, before, after, velocity, out):
    level = pl.program_id(0)
    tracers = field.shape[0]
    levels = velocity.shape[1]
    padded = []
    for which in range(2):
        at = 3 * tracers + which * levels + 1 + level
        padded.append(jnp.concatenate([before[at], velocity[which, 1 + level], after[at]], axis=0))

    def body(tracer, carry):
        at = 3 * tracer + level
        value = jnp.concatenate([before[at], field[tracer, 0], after[at]], axis=0)
        for _ in range(2):
            value = substep(value, *padded)
        out[tracer, 0] = value[2:6]
        return carry

    lax.fori_loop(0, tracers, body, 0)


def surface_kernel(velocity, before_v, after_v, first, last, before, after, whole, out):
    del whole
    tracers = first.shape[0]
    levels = velocity.shape[1]
    padded = []
    for which in range(2):
        at = 3 * tracers + which * levels
        padded.append(jnp.concatenate([before_v[at], velocity[which, 0], after_v[at]], axis=0))

    def body(tracer, carry):
        value = jnp.concatenate([before[tracer], first[tracer], last[tracer], after[tracer]], axis=0)
        for _ in range(2):
            value = substep(value, *padded)
        out[tracer, 0] = value[2:6]
        return carry

    lax.fori_loop(0, tracers, body, 0)


def whole_spec(shape):
    return pl.BlockSpec(shape, lambda *_: (0,) * len(shape))


def upper_levels(field, before, after, velocity):
    tracers, levels, rows, width = field.shape
    block = (tracers, 1, rows, width)
    return pl.pallas_call(
        upper_kernel,
        grid=(levels - 1,),
        out_shape=jax.ShapeDtypeStruct(field.shape, jnp.float32),
        in_specs=[
            pl.BlockSpec(block, lambda level: (0, level + 1, 0, 0)),
            whole_spec(before.shape),
            whole_spec(after.shape),
            whole_spec(velocity.shape),
        ],
        out_specs=pl.BlockSpec(block, lambda level: (0, level + 1, 0, 0)),
        compiler_params=pltpu.CompilerParams(vmem_limit_bytes=VMEM_LIMIT),
        cost_estimate=pl.CostEstimate(flops=10**9, bytes_accessed=3 * 10**6, transcendentals=0),
        name="upper_levels",
    )(field, before, after, velocity)


def surface_level(velocity, before_v, after_v, first, last, before, after, whole):
    tracers, _, rows, width = whole.shape
    values = (velocity, before_v, after_v, first, last, before, after)
    return pl.pallas_call(
        surface_kernel,
        grid=(1,),
        out_shape=jax.ShapeDtypeStruct(whole.shape, jnp.float32),
        in_specs=[whole_spec(v.shape) for v in values] + [pl.BlockSpec(memory_space=pl.ANY)],
        out_specs=pl.BlockSpec((tracers, 1, rows, width), lambda _: (0, 0, 0, 0)),
        input_output_aliases={len(values): 0},
        compiler_params=pltpu.CompilerParams(vmem_limit_bytes=VMEM_LIMIT),
        name="surface_level",
    )(*values, whole)


def per_device(
    tracer,
    velocity,
    coupling,
    sea_mask,
    send_rows,
    send_cols,
    intersection_near,
    intersection_slot,
    intersection_weight,
):
    field = tracer[0]
    speed = velocity[0]
    tracers, levels, rows, width = field.shape
    level0 = field[:, 0]
    packed = pack(level0.reshape(tracers, rows * width), send_rows[0, 0], send_cols[0, 0])
    pieces = [moved(packed[near], 1 - near, True) for near in range(len(packed))]

    def edge(start):
        upper = lax.slice_in_dim(field[:, 1:], start, start + 2, axis=2)
        moving = lax.slice_in_dim(speed, start, start + 2, axis=2)
        return jnp.concatenate(
            [upper.reshape(tracers * (levels - 1), 2, width), moving.reshape(2 * levels, 2, width)], axis=0
        )

    before_v = moved(edge(rows - 2), 1, False)
    after_v = moved(edge(0), -1, False)

    shared = (
        intersection_near[0],
        intersection_slot[0],
        intersection_weight[0],
        level0,
        coupling[0],
        sea_mask[0],
    )
    first = remap((0, 1), pieces, *shared)
    after = moved(first, -1, False)
    last = remap((2, 3), pieces, *shared)
    before = moved(last, 1, False)
    whole = upper_levels(field, before_v, after_v, speed)
    return surface_level(speed, before_v, after_v, first, last, before, after, whole)[None]


def solution(mesh):
    in_specs = (
        P("comp", None, None, "tile", None),
        P("comp", None, None, "tile", None),
        P("comp", None, "tile", None),
        P("comp", "tile", None),
        P("comp", "tile", None, None),
        P("comp", "tile", None, None),
        P("comp", None, "tile", None),
        P("comp", None, "tile", None),
        P("comp", None, "tile", None),
    )
    out_specs = P("comp", None, None, "tile", None)
    return jax.shard_map(
        per_device, mesh=mesh, in_specs=in_specs, out_specs=out_specs, check_vma=False
    )
```

```python
import functools

import jax
import jax.numpy as jnp
from jax import lax
from jax.experimental import pallas as pl
from jax.experimental.pallas import tpu as pltpu
from jax.sharding import PartitionSpec as P

diffusion = 0.12
LOW = 128
VMEM_LIMIT = 48 * 2**20
PACK_ORDER = (3, 0, 2, 1)
UNROLL = 4


def moved(value, steps, swap):
    tiles = lax.axis_size("tile")
    pairs = []
    for comp in range(lax.axis_size("comp")):
        for tile in range(tiles):
            target = (comp ^ 1 if swap else comp) * tiles + (tile + steps) % tiles
            pairs.append((comp * tiles + tile, target))
    return lax.ppermute(value, ("comp", "tile"), pairs)


def put_table(table, tracers, first, count, part):
    for high in range(count):
        value = part(high)
        leading = value.astype(jnp.bfloat16)
        rest = (value - leading.astype(jnp.float32)).astype(jnp.bfloat16)
        row = (first + high) * tracers
        table[row : row + tracers, :] = jnp.concatenate([leading, rest], axis=1)


def one_hot(low):
    width = low.shape[1]
    position = lax.broadcasted_iota(jnp.int32, (LOW, width), 0).astype(jnp.float32).astype(jnp.bfloat16)
    wanted = jnp.broadcast_to(low.astype(jnp.float32), (16, width)).astype(jnp.bfloat16)
    wanted = jnp.concatenate([wanted] * (LOW // 16), axis=0)
    return jnp.where(position == wanted, jnp.bfloat16(1), jnp.bfloat16(0))


def chosen(values, high):
    bit = 0
    while len(values) > 1:
        odd = ((high >> bit) & 1) == 1
        values = [jnp.where(odd, values[i + 1], values[i]) for i in range(0, len(values), 2)]
        bit += 1
    return values[0]


def looked_up(table, entry, tracers):
    width = entry.shape[1]
    highs = table.shape[0] // tracers
    hot = one_hot(entry & (LOW - 1))
    hot = jnp.concatenate([hot, hot], axis=0)
    product = jnp.dot(table[...], hot, preferred_element_type=jnp.float32)
    high = jnp.broadcast_to(entry // LOW, (tracers, width))
    return chosen([product[tracers * h : tracers * (h + 1)] for h in range(highs)], high)


def pack_kernel(field, rows, cols, *rest):
    outs, table = rest[:-1], rest[-1]
    tracers, _, grid_rows, width = field.shape
    per_row = width // LOW

    def part(high):
        low = high % per_row * LOW
        return field[:, 0, high // per_row, low : low + LOW]

    put_table(table, tracers, 0, grid_rows * per_row, part)
    block = 512
    for near in PACK_ORDER:
        for start in range(0, rows.shape[1], block):
            at = slice(start, start + block)
            entry = rows[near : near + 1, at] * width + cols[near : near + 1, at]
            outs[near][:, at] = looked_up(table, entry, tracers)


def level_spec(field):
    tracers, _, rows, width = field.shape
    return pl.BlockSpec((tracers, 1, rows, width), lambda *_: (0, 0, 0, 0))


def pack(field, rows, cols):
    tracers, _, grid_rows, width = field.shape
    neighbours, capacity = rows.shape
    piece = (tracers, capacity)
    return pl.pallas_call(
        pack_kernel,
        grid=(1,),
        in_specs=[level_spec(field), whole_spec(rows.shape), whole_spec(cols.shape)],
        out_specs=[whole_spec(piece)] * neighbours,
        out_shape=[jax.ShapeDtypeStruct(piece, jnp.float32)] * neighbours,
        scratch_shapes=[pltpu.VMEM((grid_rows * width // LOW * tracers, 2 * LOW), jnp.bfloat16)],
        compiler_params=pltpu.CompilerParams(vmem_limit_bytes=VMEM_LIMIT),
        cost_estimate=pl.CostEstimate(flops=4 * 10**9, bytes_accessed=10**6, transcendentals=0),
        name="pack",
    )(field, rows, cols)


def remap_kernel(grid_rows, near, slot, weight, field, coupling, mask, *rest):
    pieces, out, table = rest[:-2], rest[-2], rest[-1]
    tracers, capacity = pieces[0].shape
    width = field.shape[3]
    for index, piece in enumerate(pieces):
        put_table(
            table,
            tracers,
            index * (capacity // LOW),
            capacity // LOW,
            lambda high, piece=piece: piece[:, high * LOW : (high + 1) * LOW],
        )
    block = 512
    for place, row in enumerate(grid_rows):

        def body(step, carry, place=place, row=row):
            at = pl.ds(pl.multiple_of(step * block, block), block)
            total = jnp.zeros((tracers, block), jnp.float32)
            for k in range(near.shape[0]):
                entry = near[k, row : row + 1, at] * capacity + slot[k, row : row + 1, at]
                total = total + weight[k, row : row + 1, at] * looked_up(table, entry, tracers)
            own = field[:, 0, row, at]
            wet = mask[row : row + 1, at].astype(jnp.float32)
            out[:, place, at] = own + coupling[:, row, at] * wet * (total - own)
            return carry

        lax.fori_loop(0, width // block, body, 0)


def remap(grid_rows, pieces, near, slot, weight, field, coupling, mask):
    tracers, capacity = pieces[0].shape
    out = (tracers, len(grid_rows), field.shape[3])
    specs = [whole_spec(v.shape) for v in (near, slot, weight, coupling, mask, *pieces)]
    specs.insert(3, level_spec(field))
    return pl.pallas_call(
        functools.partial(remap_kernel, grid_rows),
        grid=(1,),
        in_specs=specs,
        out_specs=whole_spec(out),
        out_shape=jax.ShapeDtypeStruct(out, jnp.float32),
        scratch_shapes=[pltpu.VMEM((len(pieces) * capacity // LOW * tracers, 2 * LOW), jnp.bfloat16)],
        compiler_params=pltpu.CompilerParams(vmem_limit_bytes=VMEM_LIMIT),
        cost_estimate=pl.CostEstimate(flops=15 * 10**9, bytes_accessed=10**6, transcendentals=0),
        name="remap",
    )(near, slot, weight, field, coupling, mask, *pieces)


def set_factors(factors, speed_x, speed_y):
    factors[0] = diffusion - 0.5 * speed_x
    factors[1] = diffusion + 0.5 * speed_x
    factors[2] = diffusion - 0.5 * speed_y
    factors[3] = diffusion + 0.5 * speed_y


def substep(field, factors):
    rows, width = field.shape
    east = pltpu.roll(field, rows - 1, axis=0)
    west = pltpu.roll(field, 1, axis=0)
    north = pltpu.roll(field, width - 1, axis=1)
    south = pltpu.roll(field, 1, axis=1)
    return (
        (1 - 4 * diffusion) * field
        + (factors[0] * east + factors[1] * west)
        + (factors[2] * north + factors[3] * south)
    )


def transported(tracers, factors, padded, store):
    def body(step, carry):
        for offset in range(UNROLL):
            tracer = step * UNROLL + offset
            store(tracer, substep(substep(padded(tracer), factors), factors)[:4])
        return carry

    lax.fori_loop(0, tracers // UNROLL, body, 0)


def upper_kernel(field, before, after, velocity, out, factors):
    level = pl.program_id(0)
    tracers = field.shape[0]
    levels = velocity.shape[1]
    speeds = []
    for which in range(2):
        at = 3 * tracers + which * levels + 1 + level
        speeds.append(jnp.concatenate([velocity[which, 1 + level], after[at], before[at]], axis=0))
    set_factors(factors, *speeds)

    def padded(tracer):
        at = 3 * tracer + level
        return jnp.concatenate([field[tracer, 0], after[at], before[at]], axis=0)

    def store(tracer, value):
        out[tracer, 0] = value

    transported(tracers, factors, padded, store)


def surface_kernel(velocity, before_v, after_v, first, last, before, after, whole, out, factors):
    del whole
    tracers = first.shape[0]
    levels = velocity.shape[1]
    speeds = []
    for which in range(2):
        at = 3 * tracers + which * levels
        speeds.append(jnp.concatenate([velocity[which, 0], after_v[at], before_v[at]], axis=0))
    set_factors(factors, *speeds)

    def padded(tracer):
        return jnp.concatenate([first[tracer], last[tracer], after[tracer], before[tracer]], axis=0)

    def store(tracer, value):
        out[tracer, 0] = value

    transported(tracers, factors, padded, store)


def whole_spec(shape):
    return pl.BlockSpec(shape, lambda *_: (0,) * len(shape))


def upper_levels(field, before, after, velocity):
    tracers, levels, rows, width = field.shape
    block = (tracers, 1, rows, width)
    return pl.pallas_call(
        upper_kernel,
        grid=(levels - 1,),
        out_shape=jax.ShapeDtypeStruct(field.shape, jnp.float32),
        in_specs=[
            pl.BlockSpec(block, lambda level: (0, level + 1, 0, 0)),
            whole_spec(before.shape),
            whole_spec(after.shape),
            whole_spec(velocity.shape),
        ],
        out_specs=pl.BlockSpec(block, lambda level: (0, level + 1, 0, 0)),
        scratch_shapes=[pltpu.VMEM((4, 8, width), jnp.float32)],
        compiler_params=pltpu.CompilerParams(vmem_limit_bytes=VMEM_LIMIT),
        cost_estimate=pl.CostEstimate(flops=10**9, bytes_accessed=3 * 10**6, transcendentals=0),
        name="upper_levels",
    )(field, before, after, velocity)


def surface_level(velocity, before_v, after_v, first, last, before, after, whole):
    tracers, _, rows, width = whole.shape
    values = (velocity, before_v, after_v, first, last, before, after)
    return pl.pallas_call(
        surface_kernel,
        grid=(1,),
        out_shape=jax.ShapeDtypeStruct(whole.shape, jnp.float32),
        in_specs=[whole_spec(v.shape) for v in values] + [pl.BlockSpec(memory_space=pl.ANY)],
        out_specs=pl.BlockSpec((tracers, 1, rows, width), lambda _: (0, 0, 0, 0)),
        input_output_aliases={len(values): 0},
        scratch_shapes=[pltpu.VMEM((4, 8, width), jnp.float32)],
        compiler_params=pltpu.CompilerParams(vmem_limit_bytes=VMEM_LIMIT),
        name="surface_level",
    )(*values, whole)


def per_device(
    tracer,
    velocity,
    coupling,
    sea_mask,
    send_rows,
    send_cols,
    intersection_near,
    intersection_slot,
    intersection_weight,
):
    field = tracer[0]
    speed = velocity[0]
    tracers, levels, rows, width = field.shape
    packed = pack(field, send_rows[0, 0], send_cols[0, 0])
    pieces = [moved(packed[near], 1 - near, True) for near in range(len(packed))]

    def edge(start):
        upper = lax.slice_in_dim(field[:, 1:], start, start + 2, axis=2)
        moving = lax.slice_in_dim(speed, start, start + 2, axis=2)
        return jnp.concatenate(
            [upper.reshape(tracers * (levels - 1), 2, width), moving.reshape(2 * levels, 2, width)], axis=0
        )

    before_v = moved(edge(rows - 2), 1, False)
    after_v = moved(edge(0), -1, False)

    shared = (
        intersection_near[0],
        intersection_slot[0],
        intersection_weight[0],
        field,
        coupling[0],
        sea_mask[0],
    )
    first = remap((0, 1), pieces, *shared)
    after = moved(first, -1, False)
    last = remap((2, 3), pieces, *shared)
    before = moved(last, 1, False)
    whole = upper_levels(field, before_v, after_v, speed)
    return surface_level(speed, before_v, after_v, first, last, before, after, whole)[None]


def solution(mesh):
    in_specs = (
        P("comp", None, None, "tile", None),
        P("comp", None, None, "tile", None),
        P("comp", None, "tile", None),
        P("comp", "tile", None),
        P("comp", "tile", None, None),
        P("comp", "tile", None, None),
        P("comp", None, "tile", None),
        P("comp", None, "tile", None),
        P("comp", None, "tile", None),
    )
    out_specs = P("comp", None, None, "tile", None)
    return jax.shard_map(
        per_device, mesh=mesh, in_specs=in_specs, out_specs=out_specs, check_vma=False
    )
```

```python
import functools

import jax
import jax.numpy as jnp
from jax import lax
from jax.experimental import pallas as pl
from jax.experimental.pallas import tpu as pltpu
from jax.sharding import PartitionSpec as P

diffusion = 0.12
LOW = 128
VMEM_LIMIT = 48 * 2**20
UNROLL = 4


def moved(value, steps, swap):
    tiles = lax.axis_size("tile")
    pairs = []
    for comp in range(lax.axis_size("comp")):
        for tile in range(tiles):
            target = (comp ^ 1 if swap else comp) * tiles + (tile + steps) % tiles
            pairs.append((comp * tiles + tile, target))
    return lax.ppermute(value, ("comp", "tile"), pairs)


def put_table(table, tracers, first, count, part):
    for high in range(count):
        value = part(high)
        leading = value.astype(jnp.bfloat16)
        rest = (value - leading.astype(jnp.float32)).astype(jnp.bfloat16)
        row = (first + high) * tracers
        table[row : row + tracers, :] = jnp.concatenate([leading, rest], axis=1)


def one_hot(low):
    width = low.shape[1]
    position = lax.broadcasted_iota(jnp.int32, (LOW, width), 0).astype(jnp.float32).astype(jnp.bfloat16)
    wanted = jnp.broadcast_to(low.astype(jnp.float32), (16, width)).astype(jnp.bfloat16)
    wanted = jnp.concatenate([wanted] * (LOW // 16), axis=0)
    return jnp.where(position == wanted, jnp.bfloat16(1), jnp.bfloat16(0))


def chosen(values, high):
    bit = 0
    while len(values) > 1:
        odd = ((high >> bit) & 1) == 1
        values = [jnp.where(odd, values[i + 1], values[i]) for i in range(0, len(values), 2)]
        bit += 1
    return values[0]


def looked_up(table, entry, tracers):
    width = entry.shape[1]
    highs = table.shape[0] // tracers
    hot = one_hot(entry & (LOW - 1))
    hot = jnp.concatenate([hot, hot], axis=0)
    product = jnp.dot(table[...], hot, preferred_element_type=jnp.float32)
    high = jnp.broadcast_to(entry // LOW, (tracers, width))
    return chosen([product[tracers * h : tracers * (h + 1)] for h in range(highs)], high)


def pack_kernel(field, speed, rows, cols, before_v, after_v, *rest):
    outs, (table, level0, upper, moving, row_list, col_list, sems) = rest[:-7], rest[-7:]
    tracers, levels, grid_rows, width = field.shape
    copies = [
        pltpu.make_async_copy(source, target, sems.at[i])
        for i, (source, target) in enumerate(
            (
                (field.at[:, 0], level0),
                (rows, row_list),
                (cols, col_list),
                (speed, moving),
                (field.at[:, pl.ds(1, levels - 1)], upper),
            )
        )
    ]
    for copy in copies:
        copy.start()
    for copy in copies[:3]:
        copy.wait()
    per_row = width // LOW

    def part(high):
        low = high % per_row * LOW
        return level0[:, high // per_row, low : low + LOW]

    put_table(table, tracers, 0, grid_rows * per_row, part)
    block = 512
    for near in range(rows.shape[0]):
        for start in range(0, rows.shape[1], block):
            at = slice(start, start + block)
            entry = row_list[near : near + 1, at] * width + col_list[near : near + 1, at]
            outs[near][:, at] = looked_up(table, entry, tracers)
    for copy in copies[3:]:
        copy.wait()
    for which in range(2):
        for level in range(levels):
            at = (levels - 1) * tracers + which * levels + level
            after_v[at] = moving[which, level, :2]
            before_v[at] = moving[which, level, grid_rows - 2 :]

    def body(tracer, carry):
        for level in range(levels - 1):
            at = (levels - 1) * tracer + level
            after_v[at] = upper[tracer, level, :2]
            before_v[at] = upper[tracer, level, grid_rows - 2 :]
        return carry

    lax.fori_loop(0, tracers, body, 0, unroll=4)


def level_spec(field):
    tracers, _, rows, width = field.shape
    return pl.BlockSpec((tracers, 1, rows, width), lambda *_: (0, 0, 0, 0))


def pack(field, speed, rows, cols):
    tracers, levels, grid_rows, width = field.shape
    neighbours, capacity = rows.shape
    edge = jax.ShapeDtypeStruct(((levels - 1) * tracers + 2 * levels, 2, width), jnp.float32)
    piece = jax.ShapeDtypeStruct((tracers, capacity), jnp.float32)
    return pl.pallas_call(
        pack_kernel,
        in_specs=[pl.BlockSpec(memory_space=pltpu.HBM)] * 4,
        out_shape=[edge, edge] + [piece] * neighbours,
        scratch_shapes=[
            pltpu.VMEM((grid_rows * width // LOW * tracers, 2 * LOW), jnp.bfloat16),
            pltpu.VMEM((tracers, grid_rows, width), jnp.float32),
            pltpu.VMEM((tracers, levels - 1, grid_rows, width), jnp.float32),
            pltpu.VMEM(speed.shape, jnp.float32),
            pltpu.VMEM(rows.shape, jnp.int32),
            pltpu.VMEM(cols.shape, jnp.int32),
            pltpu.SemaphoreType.DMA((5,)),
        ],
        compiler_params=pltpu.CompilerParams(vmem_limit_bytes=60 * 2**20),
        cost_estimate=pl.CostEstimate(flops=4 * 10**9, bytes_accessed=10**6, transcendentals=0),
        name="pack",
    )(field, speed, rows, cols)


def remap_kernel(grid_rows, near, slot, weight, field, coupling, mask, *rest):
    pieces, edges, out, table = rest[:4], rest[4:-2], rest[-2], rest[-1]
    tracers, capacity = pieces[0].shape
    for edge in edges:
        out[tracers:] = edge[...]
    width = field.shape[3]
    for index, piece in enumerate(pieces):
        put_table(
            table,
            tracers,
            index * (capacity // LOW),
            capacity // LOW,
            lambda high, piece=piece: piece[:, high * LOW : (high + 1) * LOW],
        )
    block = 512
    for place, row in enumerate(grid_rows):

        def body(step, carry, place=place, row=row):
            at = pl.ds(pl.multiple_of(step * block, block), block)
            total = jnp.zeros((tracers, block), jnp.float32)
            for k in range(near.shape[0]):
                entry = near[k, row : row + 1, at] * capacity + slot[k, row : row + 1, at]
                total = total + weight[k, row : row + 1, at] * looked_up(table, entry, tracers)
            own = field[:, 0, row, at]
            wet = mask[row : row + 1, at].astype(jnp.float32)
            out[:tracers, place, at] = own + coupling[:, row, at] * wet * (total - own)
            return carry

        lax.fori_loop(0, width // block, body, 0)


def remap(grid_rows, pieces, edges, near, slot, weight, field, coupling, mask):
    tracers, capacity = pieces[0].shape
    out = (tracers + sum(edge.shape[0] for edge in edges), len(grid_rows), field.shape[3])
    specs = [whole_spec(v.shape) for v in (near, slot, weight, coupling, mask, *pieces, *edges)]
    specs.insert(3, level_spec(field))
    return pl.pallas_call(
        functools.partial(remap_kernel, grid_rows),
        grid=(1,),
        in_specs=specs,
        out_specs=whole_spec(out),
        out_shape=jax.ShapeDtypeStruct(out, jnp.float32),
        scratch_shapes=[pltpu.VMEM((len(pieces) * capacity // LOW * tracers, 2 * LOW), jnp.bfloat16)],
        compiler_params=pltpu.CompilerParams(vmem_limit_bytes=VMEM_LIMIT),
        cost_estimate=pl.CostEstimate(flops=15 * 10**9, bytes_accessed=10**6, transcendentals=0),
        name="remap",
    )(near, slot, weight, field, coupling, mask, *pieces, *edges)


def set_factors(factors, speed_x, speed_y):
    factors[0] = diffusion - 0.5 * speed_x
    factors[1] = diffusion + 0.5 * speed_x
    factors[2] = diffusion - 0.5 * speed_y
    factors[3] = diffusion + 0.5 * speed_y


def substep(field, factors):
    rows, width = field.shape
    east = pltpu.roll(field, rows - 1, axis=0)
    west = pltpu.roll(field, 1, axis=0)
    north = pltpu.roll(field, width - 1, axis=1)
    south = pltpu.roll(field, 1, axis=1)
    return (
        (1 - 4 * diffusion) * field
        + (factors[0] * east + factors[1] * west)
        + (factors[2] * north + factors[3] * south)
    )


def transported(tracers, factors, padded, store):
    def body(step, carry):
        for offset in range(UNROLL):
            tracer = step * UNROLL + offset
            store(tracer, substep(substep(padded(tracer), factors), factors)[:4])
        return carry

    lax.fori_loop(0, tracers // UNROLL, body, 0)


def upper_kernel(field, before, after, velocity, out, factors):
    level = pl.program_id(0)
    tracers = field.shape[0]
    levels = velocity.shape[1]
    speeds = []
    for which in range(2):
        at = 3 * tracers + which * levels + 1 + level
        speeds.append(
            jnp.concatenate([velocity[which, 1 + level], after[at], before[tracers + at]], axis=0)
        )
    set_factors(factors, *speeds)

    def padded(tracer):
        at = 3 * tracer + level
        return jnp.concatenate([field[tracer, 0], after[at], before[tracers + at]], axis=0)

    def store(tracer, value):
        out[tracer, 0] = value

    transported(tracers, factors, padded, store)


def surface_kernel(velocity, after_v, first, last, before, after, whole, out, factors):
    del whole
    tracers = first.shape[0]
    levels = velocity.shape[1]
    speeds = []
    for which in range(2):
        at = 3 * tracers + which * levels
        speeds.append(
            jnp.concatenate([velocity[which, 0], after_v[at], before[tracers + at]], axis=0)
        )
    set_factors(factors, *speeds)

    def padded(tracer):
        return jnp.concatenate([first[tracer], last[tracer], after[tracer], before[tracer]], axis=0)

    def store(tracer, value):
        out[tracer, 0] = value

    transported(tracers, factors, padded, store)


def whole_spec(shape):
    return pl.BlockSpec(shape, lambda *_: (0,) * len(shape))


def upper_levels(field, before, after, velocity):
    tracers, levels, rows, width = field.shape
    block = (tracers, 1, rows, width)
    return pl.pallas_call(
        upper_kernel,
        grid=(levels - 1,),
        out_shape=jax.ShapeDtypeStruct(field.shape, jnp.float32),
        in_specs=[
            pl.BlockSpec(block, lambda level: (0, level + 1, 0, 0)),
            whole_spec(before.shape),
            whole_spec(after.shape),
            whole_spec(velocity.shape),
        ],
        out_specs=pl.BlockSpec(block, lambda level: (0, level + 1, 0, 0)),
        scratch_shapes=[pltpu.VMEM((4, 8, width), jnp.float32)],
        compiler_params=pltpu.CompilerParams(vmem_limit_bytes=VMEM_LIMIT),
        cost_estimate=pl.CostEstimate(flops=10**6, bytes_accessed=10**5, transcendentals=0),
        name="upper_levels",
    )(field, before, after, velocity)


def surface_level(velocity, after_v, first, last, before, after, whole):
    tracers, _, rows, width = whole.shape
    values = (velocity, after_v, first, last, before, after)
    return pl.pallas_call(
        surface_kernel,
        grid=(1,),
        out_shape=jax.ShapeDtypeStruct(whole.shape, jnp.float32),
        in_specs=[whole_spec(v.shape) for v in values] + [pl.BlockSpec(memory_space=pl.ANY)],
        out_specs=pl.BlockSpec((tracers, 1, rows, width), lambda _: (0, 0, 0, 0)),
        input_output_aliases={len(values): 0},
        scratch_shapes=[pltpu.VMEM((4, 8, width), jnp.float32)],
        compiler_params=pltpu.CompilerParams(vmem_limit_bytes=VMEM_LIMIT),
        name="surface_level",
    )(*values, whole)


def per_device(
    tracer,
    velocity,
    coupling,
    sea_mask,
    send_rows,
    send_cols,
    intersection_near,
    intersection_slot,
    intersection_weight,
):
    field = tracer[0]
    speed = velocity[0]
    tracers, levels, rows, width = field.shape
    before_v, after_v, *packed = pack(field, speed, send_rows[0, 0], send_cols[0, 0])
    pieces = [moved(packed[near], 1 - near, True) for near in range(len(packed))]
    after_v = moved(after_v, -1, False)
    shared = (
        intersection_near[0],
        intersection_slot[0],
        intersection_weight[0],
        field,
        coupling[0],
        sea_mask[0],
    )
    last = remap((2, 3), pieces, [before_v], *shared)
    before = moved(last, 1, False)
    pieces, last = lax.optimization_barrier((pieces, last))
    first = remap((0, 1), pieces, [], *shared)
    after = moved(first, -1, False)
    whole = upper_levels(field, before, after_v, speed)
    return surface_level(speed, after_v, first, last, before, after, whole)[None]


def solution(mesh):
    in_specs = (
        P("comp", None, None, "tile", None),
        P("comp", None, None, "tile", None),
        P("comp", None, "tile", None),
        P("comp", "tile", None),
        P("comp", "tile", None, None),
        P("comp", "tile", None, None),
        P("comp", None, "tile", None),
        P("comp", None, "tile", None),
        P("comp", None, "tile", None),
    )
    out_specs = P("comp", None, None, "tile", None)
    return jax.shard_map(
        per_device, mesh=mesh, in_specs=in_specs, out_specs=out_specs, check_vma=False
    )
```

```python
import functools

import jax
import jax.numpy as jnp
from jax import lax
from jax.experimental import pallas as pl
from jax.experimental.pallas import tpu as pltpu
from jax.sharding import PartitionSpec as P

diffusion = 0.12
LOW = 128
BLOCK = 512
UNROLL = 4
VMEM_LIMIT = 48 * 2**20
FULL_VMEM = 60 * 2**20
SMALL_COST = pl.CostEstimate(flops=10**6, bytes_accessed=10**5, transcendentals=0)


def moved(value, steps, swap):
    tiles = lax.axis_size("tile")
    pairs = []
    for comp in range(lax.axis_size("comp")):
        for tile in range(tiles):
            target = (comp ^ 1 if swap else comp) * tiles + (tile + steps) % tiles
            pairs.append((comp * tiles + tile, target))
    return lax.ppermute(value, ("comp", "tile"), pairs)


def put_table(table, tracers, first, count, part):
    for high in range(count):
        value = part(high)
        leading = value.astype(jnp.bfloat16)
        rest = (value - leading.astype(jnp.float32)).astype(jnp.bfloat16)
        row = (first + high) * tracers
        table[row : row + tracers, :] = jnp.concatenate([leading, rest], axis=1)


def one_hot(low):
    width = low.shape[1]
    position = lax.broadcasted_iota(jnp.int32, (LOW, width), 0).astype(jnp.float32).astype(jnp.bfloat16)
    wanted = jnp.broadcast_to(low.astype(jnp.float32), (16, width)).astype(jnp.bfloat16)
    wanted = jnp.concatenate([wanted] * (LOW // 16), axis=0)
    return jnp.where(position == wanted, jnp.bfloat16(1), jnp.bfloat16(0))


def chosen(values, high):
    bit = 0
    while len(values) > 1:
        odd = ((high >> bit) & 1) == 1
        values = [jnp.where(odd, values[i + 1], values[i]) for i in range(0, len(values), 2)]
        bit += 1
    return values[0]


def low_product(table, entry, tracers):
    hot = one_hot(entry & (LOW - 1))
    hot = jnp.concatenate([hot, hot], axis=0)
    product = jnp.dot(table[...], hot, preferred_element_type=jnp.float32)
    return [product[at : at + tracers] for at in range(0, table.shape[0], tracers)]


def high_part(entry, tracers):
    return jnp.broadcast_to(entry // LOW, (tracers, entry.shape[1]))


def started(pairs, sems):
    copies = [pltpu.make_async_copy(source, target, sems.at[i]) for i, (source, target) in enumerate(pairs)]
    for copy in copies:
        copy.start()
    return copies


def edges_kernel(field, speed, before_v, after_v, upper, moving, sems):
    tracers, levels, grid_rows, _ = field.shape
    for copy in started(((speed, moving), (field.at[:, pl.ds(1, levels - 1)], upper)), sems):
        copy.wait()
    for which in range(2):
        for level in range(levels):
            at = (levels - 1) * tracers + which * levels + level
            after_v[at] = moving[which, level, :2]
            before_v[at] = moving[which, level, grid_rows - 2 :]

    def body(tracer, carry):
        for level in range(levels - 1):
            at = (levels - 1) * tracer + level
            after_v[at] = upper[tracer, level, :2]
            before_v[at] = upper[tracer, level, grid_rows - 2 :]
        return carry

    lax.fori_loop(0, tracers, body, 0, unroll=4)


def edges(field, speed):
    tracers, levels, grid_rows, width = field.shape
    edge = jax.ShapeDtypeStruct(((levels - 1) * tracers + 2 * levels, 2, width), jnp.float32)
    return pl.pallas_call(
        edges_kernel,
        in_specs=[pl.BlockSpec(memory_space=pltpu.HBM)] * 2,
        out_shape=[edge, edge],
        scratch_shapes=[
            pltpu.VMEM((tracers, levels - 1, grid_rows, width), jnp.float32),
            pltpu.VMEM(speed.shape, jnp.float32),
            pltpu.SemaphoreType.DMA((2,)),
        ],
        compiler_params=pltpu.CompilerParams(vmem_limit_bytes=FULL_VMEM),
        cost_estimate=SMALL_COST,
        name="edges",
    )(field, speed)


def pack_kernel(field, rows, cols, *rest):
    outs, (table, level0, row_list, col_list, sems) = rest[:-5], rest[-5:]
    tracers, _, grid_rows, width = field.shape
    for copy in started(((field.at[:, 0], level0), (rows, row_list), (cols, col_list)), sems):
        copy.wait()
    per_row = width // LOW

    def part(high):
        low = high % per_row * LOW
        return level0[:, high // per_row, low : low + LOW]

    put_table(table, tracers, 0, grid_rows * per_row, part)
    for near in range(rows.shape[0]):
        for start in range(0, rows.shape[1], BLOCK):
            at = slice(start, start + BLOCK)
            entry = row_list[near : near + 1, at] * width + col_list[near : near + 1, at]
            product = low_product(table, entry, tracers)
            outs[near][:, at] = chosen(product, high_part(entry, tracers))


def level_spec(field):
    tracers, _, rows, width = field.shape
    return pl.BlockSpec((tracers, 1, rows, width), lambda *_: (0, 0, 0, 0))


def pack(field, rows, cols):
    tracers, _, grid_rows, width = field.shape
    neighbours, capacity = rows.shape
    piece = jax.ShapeDtypeStruct((tracers, capacity), jnp.float32)
    return pl.pallas_call(
        pack_kernel,
        in_specs=[pl.BlockSpec(memory_space=pltpu.HBM)] * 3,
        out_shape=[piece] * neighbours,
        scratch_shapes=[
            pltpu.VMEM((grid_rows * width // LOW * tracers, 2 * LOW), jnp.bfloat16),
            pltpu.VMEM((tracers, grid_rows, width), jnp.float32),
            pltpu.VMEM(rows.shape, jnp.int32),
            pltpu.VMEM(cols.shape, jnp.int32),
            pltpu.SemaphoreType.DMA((3,)),
        ],
        compiler_params=pltpu.CompilerParams(vmem_limit_bytes=FULL_VMEM),
        cost_estimate=SMALL_COST,
        name="pack",
    )(field, rows, cols)


def added_reads(sources, near, slot, weight, table, tracers, row, at):
    total = None
    for k in range(near.shape[0]):
        which = near[k, row : row + 1, at]
        entry = slot[k, row : row + 1, at]
        product = low_product(table, entry, tracers)
        high = high_part(entry, tracers)
        count = len(product) // len(sources)
        wide = jnp.broadcast_to(which, high.shape)
        read = chosen(product[:count], high)
        inside = which == sources[0]
        for rank in range(1, len(sources)):
            part = chosen(product[rank * count : (rank + 1) * count], high)
            read = jnp.where(wide == sources[rank], part, read)
            inside = inside | (which == sources[rank])
        term = jnp.where(inside, weight[k, row : row + 1, at], 0.0) * read
        total = term if total is None else total + term
    return total


def put_pieces(table, pieces):
    tracers, capacity = pieces[0].shape
    count = capacity // LOW
    for index, piece in enumerate(pieces):
        put_table(
            table, tracers, index * count, count, lambda high, piece=piece: piece[:, high * LOW : (high + 1) * LOW]
        )


def near_kernel(sources, near, slot, weight, piece, out, table):
    tracers = piece.shape[0]
    put_pieces(table, [piece])
    width = near.shape[2]
    for row in range(near.shape[1]):

        def body(step, carry, row=row):
            at = pl.ds(pl.multiple_of(step * BLOCK, BLOCK), BLOCK)
            out[:, row, at] = added_reads(sources, near, slot, weight, table, tracers, row, at)
            return carry

        lax.fori_loop(0, width // BLOCK, body, 0)


def remap_near(source, near, slot, weight, piece):
    tracers, capacity = piece.shape
    _, rows, width = near.shape
    return pl.pallas_call(
        functools.partial(near_kernel, (source,)),
        out_shape=jax.ShapeDtypeStruct((tracers, rows, width), jnp.float32),
        scratch_shapes=[pltpu.VMEM((capacity // LOW * tracers, 2 * LOW), jnp.bfloat16)],
        compiler_params=pltpu.CompilerParams(vmem_limit_bytes=VMEM_LIMIT),
        cost_estimate=SMALL_COST,
        name="remap_near",
    )(near, slot, weight, piece)


def remap_kernel(sources, grid_rows, near, slot, weight, field, coupling, mask, partial, *rest):
    pieces, (out, table) = rest[:-2], rest[-2:]
    tracers = field.shape[0]
    put_pieces(table, pieces)
    for place, row in enumerate(grid_rows):

        def body(step, carry, place=place, row=row):
            at = pl.ds(pl.multiple_of(step * BLOCK, BLOCK), BLOCK)
            total = added_reads(sources, near, slot, weight, table, tracers, row, at)
            total = total + partial[:, row, at]
            own = field[:, 0, row, at]
            wet = mask[row : row + 1, at].astype(jnp.float32)
            out[:, place, at] = own + coupling[:, row, at] * wet * (total - own)
            return carry

        lax.fori_loop(0, field.shape[3] // BLOCK, body, 0)


def remap(sources, grid_rows, pieces, near, slot, weight, field, coupling, mask, partial):
    tracers, capacity = pieces[0].shape
    out = (tracers, len(grid_rows), field.shape[3])
    specs = [whole_spec(v.shape) for v in (near, slot, weight, coupling, mask, partial, *pieces)]
    specs.insert(3, level_spec(field))
    return pl.pallas_call(
        functools.partial(remap_kernel, sources, grid_rows),
        grid=(1,),
        in_specs=specs,
        out_specs=whole_spec(out),
        out_shape=jax.ShapeDtypeStruct(out, jnp.float32),
        scratch_shapes=[pltpu.VMEM((len(pieces) * capacity // LOW * tracers, 2 * LOW), jnp.bfloat16)],
        compiler_params=pltpu.CompilerParams(vmem_limit_bytes=VMEM_LIMIT),
        cost_estimate=pl.CostEstimate(flops=15 * 10**9, bytes_accessed=10**6, transcendentals=0),
        name="remap",
    )(near, slot, weight, field, coupling, mask, partial, *pieces)


def set_factors(factors, speed_x, speed_y):
    factors[0] = diffusion - 0.5 * speed_x
    factors[1] = diffusion + 0.5 * speed_x
    factors[2] = diffusion - 0.5 * speed_y
    factors[3] = diffusion + 0.5 * speed_y


def substep(field, factors):
    rows, width = field.shape
    east = pltpu.roll(field, rows - 1, axis=0)
    west = pltpu.roll(field, 1, axis=0)
    north = pltpu.roll(field, width - 1, axis=1)
    south = pltpu.roll(field, 1, axis=1)
    return (
        (1 - 4 * diffusion) * field
        + (factors[0] * east + factors[1] * west)
        + (factors[2] * north + factors[3] * south)
    )


def transported(tracers, factors, padded, store):
    def body(step, carry):
        for offset in range(UNROLL):
            tracer = step * UNROLL + offset
            store(tracer, substep(substep(padded(tracer), factors), factors)[:4])
        return carry

    lax.fori_loop(0, tracers // UNROLL, body, 0)


def upper_kernel(field, before_v, after_v, velocity, out, factors):
    level = pl.program_id(0)
    tracers = field.shape[0]
    levels = velocity.shape[1]
    speeds = []
    for which in range(2):
        at = 3 * tracers + which * levels + 1 + level
        speeds.append(
            jnp.concatenate([velocity[which, 1 + level], after_v[at], before_v[at]], axis=0)
        )
    set_factors(factors, *speeds)

    def padded(tracer):
        at = 3 * tracer + level
        return jnp.concatenate([field[tracer, 0], after_v[at], before_v[at]], axis=0)

    def store(tracer, value):
        out[tracer, 0] = value

    transported(tracers, factors, padded, store)


def surface_kernel(velocity, before_v, after_v, first, last, before, after, whole, out, factors):
    del whole
    tracers = first.shape[0]
    levels = velocity.shape[1]
    speeds = []
    for which in range(2):
        at = 3 * tracers + which * levels
        speeds.append(
            jnp.concatenate([velocity[which, 0], after_v[at], before_v[at]], axis=0)
        )
    set_factors(factors, *speeds)

    def padded(tracer):
        return jnp.concatenate([first[tracer], last[tracer], after[tracer], before[tracer]], axis=0)

    def store(tracer, value):
        out[tracer, 0] = value

    transported(tracers, factors, padded, store)


def whole_spec(shape):
    return pl.BlockSpec(shape, lambda *_: (0,) * len(shape))


def upper_levels(field, before, after, velocity):
    tracers, levels, rows, width = field.shape
    block = (tracers, 1, rows, width)
    return pl.pallas_call(
        upper_kernel,
        grid=(levels - 1,),
        out_shape=jax.ShapeDtypeStruct(field.shape, jnp.float32),
        in_specs=[
            pl.BlockSpec(block, lambda level: (0, level + 1, 0, 0)),
            whole_spec(before.shape),
            whole_spec(after.shape),
            whole_spec(velocity.shape),
        ],
        out_specs=pl.BlockSpec(block, lambda level: (0, level + 1, 0, 0)),
        scratch_shapes=[pltpu.VMEM((4, 8, width), jnp.float32)],
        compiler_params=pltpu.CompilerParams(vmem_limit_bytes=VMEM_LIMIT),
        cost_estimate=SMALL_COST,
        name="upper_levels",
    )(field, before, after, velocity)


def surface_level(velocity, before_v, after_v, first, last, before, after, whole):
    tracers, _, rows, width = whole.shape
    values = (velocity, before_v, after_v, first, last, before, after)
    return pl.pallas_call(
        surface_kernel,
        grid=(1,),
        out_shape=jax.ShapeDtypeStruct(whole.shape, jnp.float32),
        in_specs=[whole_spec(v.shape) for v in values] + [pl.BlockSpec(memory_space=pl.ANY)],
        out_specs=pl.BlockSpec((tracers, 1, rows, width), lambda _: (0, 0, 0, 0)),
        input_output_aliases={len(values): 0},
        scratch_shapes=[pltpu.VMEM((4, 8, width), jnp.float32)],
        compiler_params=pltpu.CompilerParams(vmem_limit_bytes=VMEM_LIMIT),
        name="surface_level",
    )(*values, whole)


def per_device(
    tracer,
    velocity,
    coupling,
    sea_mask,
    send_rows,
    send_cols,
    intersection_near,
    intersection_slot,
    intersection_weight,
):
    field = tracer[0]
    speed = velocity[0]
    tracers, levels, rows, width = field.shape
    near, slot, weight = intersection_near[0], intersection_slot[0], intersection_weight[0]
    others = (0, 2, 3)
    before_v, after_v = edges(field, speed)
    before_v, lists = lax.optimization_barrier((before_v, (send_rows[0, 0], send_cols[0, 0])))
    packed = pack(field, *lists)
    before_v = moved(before_v, 1, False)
    pieces = [moved(packed[j], 1 - j, True) for j in range(len(packed))]
    after_v = moved(after_v, -1, False)
    partial = remap_near(1, near, slot, weight, pieces[1])
    pieces, before_v = lax.optimization_barrier(([pieces[j] for j in others], before_v))
    shared = (near, slot, weight, field, coupling[0], sea_mask[0], partial)
    last = remap(others, (2, 3), pieces, *shared)
    before = moved(last, 1, False)
    pieces, last = lax.optimization_barrier((pieces, last))
    first = remap(others, (0, 1), pieces, *shared)
    after = moved(first, -1, False)
    before_v, before = lax.optimization_barrier((before_v, before))
    whole = upper_levels(field, before_v, after_v, speed)
    return surface_level(speed, before_v, after_v, first, last, before, after, whole)[None]


def solution(mesh):
    in_specs = (
        P("comp", None, None, "tile", None),
        P("comp", None, None, "tile", None),
        P("comp", None, "tile", None),
        P("comp", "tile", None),
        P("comp", "tile", None, None),
        P("comp", "tile", None, None),
        P("comp", None, "tile", None),
        P("comp", None, "tile", None),
        P("comp", None, "tile", None),
    )
    out_specs = P("comp", None, None, "tile", None)
    return jax.shard_map(
        per_device, mesh=mesh, in_specs=in_specs, out_specs=out_specs, check_vma=False
    )
```

```python
import functools

import jax
import jax.numpy as jnp
from jax import lax
from jax.experimental import pallas as pl
from jax.experimental.pallas import tpu as pltpu
from jax.sharding import PartitionSpec as P

diffusion = 0.12
LOW = 128
BLOCK = 1024
PACK_BLOCK = 512
UNROLL = 4
VMEM_LIMIT = 48 * 2**20
FULL_VMEM = 60 * 2**20
SMALL_COST = pl.CostEstimate(flops=10**6, bytes_accessed=10**5, transcendentals=0)


def moved(value, steps, swap):
    tiles = lax.axis_size("tile")
    pairs = []
    for comp in range(lax.axis_size("comp")):
        for tile in range(tiles):
            target = (comp ^ 1 if swap else comp) * tiles + (tile + steps) % tiles
            pairs.append((comp * tiles + tile, target))
    return lax.ppermute(value, ("comp", "tile"), pairs)


def swapped(value, odd_step):
    tiles = lax.axis_size("tile")
    pairs = [(tile, (tile + (odd_step if tile % 2 else -odd_step)) % tiles) for tile in range(tiles)]
    return lax.ppermute(value, "tile", pairs)


def put_table(table, tracers, first, count, part):
    for high in range(count):
        value = part(high)
        leading = value.astype(jnp.bfloat16)
        rest = (value - leading.astype(jnp.float32)).astype(jnp.bfloat16)
        row = (first + high) * tracers
        table[row : row + tracers, :] = jnp.concatenate([leading, rest], axis=1)


def one_hot(low):
    width = low.shape[1]
    position = lax.broadcasted_iota(jnp.int32, (LOW, width), 0).astype(jnp.float32).astype(jnp.bfloat16)
    wanted = jnp.broadcast_to(low.astype(jnp.float32), (16, width)).astype(jnp.bfloat16)
    wanted = jnp.concatenate([wanted] * (LOW // 16), axis=0)
    return jnp.where(position == wanted, jnp.bfloat16(1), jnp.bfloat16(0))


def chosen(values, high):
    bit = 0
    while len(values) > 1:
        odd = ((high >> bit) & 1) == 1
        values = [jnp.where(odd, values[i + 1], values[i]) for i in range(0, len(values), 2)]
        bit += 1
    return values[0]


def low_product(table, entry, tracers):
    hot = one_hot(entry & (LOW - 1))
    hot = jnp.concatenate([hot, hot], axis=0)
    product = jnp.dot(table[...], hot, preferred_element_type=jnp.float32)
    return [product[at : at + tracers] for at in range(0, table.shape[0], tracers)]


def high_part(entry, tracers):
    return jnp.broadcast_to(entry // LOW, (tracers, entry.shape[1]))


def started(pairs, sems):
    copies = [pltpu.make_async_copy(source, target, sems.at[i]) for i, (source, target) in enumerate(pairs)]
    for copy in copies:
        copy.start()
    return copies


def edges_kernel(field, speed, before_v, after_v, upper, moving, sems):
    tracers, levels, grid_rows, _ = field.shape
    for copy in started(((speed, moving), (field.at[:, pl.ds(1, levels - 1)], upper)), sems):
        copy.wait()
    for which in range(2):
        for level in range(levels):
            at = (levels - 1) * tracers + which * levels + level
            after_v[at] = moving[which, level, :2]
            before_v[at] = moving[which, level, grid_rows - 2 :]

    def body(tracer, carry):
        for level in range(levels - 1):
            at = (levels - 1) * tracer + level
            after_v[at] = upper[tracer, level, :2]
            before_v[at] = upper[tracer, level, grid_rows - 2 :]
        return carry

    lax.fori_loop(0, tracers, body, 0, unroll=4)


def edges(field, speed):
    tracers, levels, grid_rows, width = field.shape
    edge = jax.ShapeDtypeStruct(((levels - 1) * tracers + 2 * levels, 2, width), jnp.float32)
    return pl.pallas_call(
        edges_kernel,
        in_specs=[pl.BlockSpec(memory_space=pltpu.HBM)] * 2,
        out_shape=[edge, edge],
        scratch_shapes=[
            pltpu.VMEM((tracers, levels - 1, grid_rows, width), jnp.float32),
            pltpu.VMEM(speed.shape, jnp.float32),
            pltpu.SemaphoreType.DMA((2,)),
        ],
        compiler_params=pltpu.CompilerParams(vmem_limit_bytes=FULL_VMEM),
        cost_estimate=SMALL_COST,
        name="edges",
    )(field, speed)


def pack_kernel(field, rows, cols, *rest):
    outs, table = rest[:-1], rest[-1]
    tracers, _, grid_rows, width = field.shape
    per_row = width // LOW

    def part(high):
        low = high % per_row * LOW
        return field[:, 0, high // per_row, low : low + LOW]

    put_table(table, tracers, 0, grid_rows * per_row, part)
    for near in range(rows.shape[0]):
        for start in range(0, rows.shape[1], PACK_BLOCK):
            at = slice(start, start + PACK_BLOCK)
            entry = rows[near : near + 1, at] * width + cols[near : near + 1, at]
            product = low_product(table, entry, tracers)
            outs[near][:, at] = chosen(product, high_part(entry, tracers))


def level_spec(field):
    tracers, _, rows, width = field.shape
    return pl.BlockSpec((tracers, 1, rows, width), lambda *_: (0, 0, 0, 0))


def pack(field, rows, cols):
    tracers, _, grid_rows, width = field.shape
    neighbours, capacity = rows.shape
    piece = jax.ShapeDtypeStruct((tracers, capacity), jnp.float32)
    return pl.pallas_call(
        pack_kernel,
        grid=(1,),
        in_specs=[level_spec(field), whole_spec(rows.shape), whole_spec(cols.shape)],
        out_specs=[whole_spec(piece.shape)] * neighbours,
        out_shape=[piece] * neighbours,
        scratch_shapes=[pltpu.VMEM((grid_rows * width // LOW * tracers, 2 * LOW), jnp.bfloat16)],
        compiler_params=pltpu.CompilerParams(vmem_limit_bytes=VMEM_LIMIT),
        cost_estimate=SMALL_COST,
        name="pack",
    )(field, rows, cols)


def added_reads(sources, near, slot, weight, table, tracers, row, at):
    total = None
    for k in range(near.shape[0]):
        which = near[k, pl.ds(row, 1), at]
        entry = slot[k, pl.ds(row, 1), at]
        product = low_product(table, entry, tracers)
        high = high_part(entry, tracers)
        count = len(product) // len(sources)
        wide = jnp.broadcast_to(which, high.shape)
        read = chosen(product[:count], high)
        inside = which == sources[0]
        for rank in range(1, len(sources)):
            part = chosen(product[rank * count : (rank + 1) * count], high)
            read = jnp.where(wide == sources[rank], part, read)
            inside = inside | (which == sources[rank])
        term = jnp.where(inside, weight[k, pl.ds(row, 1), at], 0.0) * read
        total = term if total is None else total + term
    return total


def put_pieces(table, pieces):
    tracers, capacity = pieces[0].shape
    count = capacity // LOW
    for index, piece in enumerate(pieces):
        put_table(
            table, tracers, index * count, count, lambda high, piece=piece: piece[:, high * LOW : (high + 1) * LOW]
        )


def near_kernel(sources, near, slot, weight, piece, out, table):
    tracers = piece.shape[0]
    put_pieces(table, [piece])
    width = near.shape[2]
    for row in range(near.shape[1]):

        def body(step, carry, row=row):
            at = pl.ds(pl.multiple_of(step * BLOCK, BLOCK), BLOCK)
            out[:, row, at] = added_reads(sources, near, slot, weight, table, tracers, row, at)
            return carry

        lax.fori_loop(0, width // BLOCK, body, 0)


def remap_near(source, near, slot, weight, piece):
    tracers, capacity = piece.shape
    _, rows, width = near.shape
    return pl.pallas_call(
        functools.partial(near_kernel, (source,)),
        out_shape=jax.ShapeDtypeStruct((tracers, rows, width), jnp.float32),
        scratch_shapes=[pltpu.VMEM((capacity // LOW * tracers, 2 * LOW), jnp.bfloat16)],
        compiler_params=pltpu.CompilerParams(vmem_limit_bytes=VMEM_LIMIT),
        cost_estimate=SMALL_COST,
        name="remap_near",
    )(near, slot, weight, piece)


def remap_kernel(sources, start, near, slot, weight, field, coupling, mask, partial, *rest):
    pieces, (out, table) = rest[:-2], rest[-2:]
    tracers = field.shape[0]
    put_pieces(table, pieces)
    for place in range(out.shape[1]):
        row = start[0] + place

        def body(step, carry, place=place, row=row):
            at = pl.ds(pl.multiple_of(step * BLOCK, BLOCK), BLOCK)
            total = added_reads(sources, near, slot, weight, table, tracers, row, at)
            total = total + partial[:, row, at]
            own = field[:, 0, row, at]
            wet = mask[pl.ds(row, 1), at].astype(jnp.float32)
            out[:, place, at] = own + coupling[:, row, at] * wet * (total - own)
            return carry

        lax.fori_loop(0, field.shape[3] // BLOCK, body, 0)


def remap(sources, start, pieces, near, slot, weight, field, coupling, mask, partial):
    tracers, capacity = pieces[0].shape
    out = (tracers, 2, field.shape[3])
    specs = [whole_spec(v.shape) for v in (near, slot, weight, coupling, mask, partial, *pieces)]
    specs.insert(3, level_spec(field))
    specs.insert(0, pl.BlockSpec(memory_space=pltpu.SMEM))
    return pl.pallas_call(
        functools.partial(remap_kernel, sources),
        grid=(1,),
        in_specs=specs,
        out_specs=whole_spec(out),
        out_shape=jax.ShapeDtypeStruct(out, jnp.float32),
        scratch_shapes=[pltpu.VMEM((len(pieces) * capacity // LOW * tracers, 2 * LOW), jnp.bfloat16)],
        compiler_params=pltpu.CompilerParams(vmem_limit_bytes=VMEM_LIMIT),
        cost_estimate=pl.CostEstimate(flops=15 * 10**9, bytes_accessed=10**6, transcendentals=0),
        name="remap",
    )(start, near, slot, weight, field, coupling, mask, partial, *pieces)


def set_factors(factors, speed_x, speed_y):
    factors[0] = diffusion - 0.5 * speed_x
    factors[1] = diffusion + 0.5 * speed_x
    factors[2] = diffusion - 0.5 * speed_y
    factors[3] = diffusion + 0.5 * speed_y


def substep(field, factors):
    rows, width = field.shape
    east = pltpu.roll(field, rows - 1, axis=0)
    west = pltpu.roll(field, 1, axis=0)
    north = pltpu.roll(field, width - 1, axis=1)
    south = pltpu.roll(field, 1, axis=1)
    return (
        (1 - 4 * diffusion) * field
        + (factors[0] * east + factors[1] * west)
        + (factors[2] * north + factors[3] * south)
    )


def transported(tracers, factors, padded, store):
    def body(step, carry):
        for offset in range(UNROLL):
            tracer = step * UNROLL + offset
            store(tracer, substep(substep(padded(tracer), factors), factors)[:4])
        return carry

    lax.fori_loop(0, tracers // UNROLL, body, 0)


def upper_kernel(field, before_v, after_v, velocity, out, factors):
    level = pl.program_id(0)
    tracers = field.shape[0]
    levels = velocity.shape[1]
    speeds = []
    for which in range(2):
        at = 3 * tracers + which * levels + 1 + level
        speeds.append(
            jnp.concatenate([velocity[which, 1 + level], after_v[at], before_v[at]], axis=0)
        )
    set_factors(factors, *speeds)

    def padded(tracer):
        at = 3 * tracer + level
        return jnp.concatenate([field[tracer, 0], after_v[at], before_v[at]], axis=0)

    def store(tracer, value):
        out[tracer, 0] = value

    transported(tracers, factors, padded, store)


def surface_kernel(start, velocity, before_v, after_v, own1, own2, got1, got2, whole, out, factors):
    del whole
    tracers = own1.shape[0]
    odd = start[0] > 0
    levels = velocity.shape[1]
    speeds = []
    for which in range(2):
        at = 3 * tracers + which * levels
        speeds.append(
            jnp.concatenate([velocity[which, 0], after_v[at], before_v[at]], axis=0)
        )
    set_factors(factors, *speeds)

    def padded(tracer):
        one, two = own1[tracer], own2[tracer]
        far1, far2 = got1[tracer], got2[tracer]
        first, last = jnp.where(odd, two, one), jnp.where(odd, one, two)
        after, before = jnp.where(odd, far1, far2), jnp.where(odd, far2, far1)
        return jnp.concatenate([first, last, after, before], axis=0)

    def store(tracer, value):
        out[tracer, 0] = value

    transported(tracers, factors, padded, store)


def whole_spec(shape):
    return pl.BlockSpec(shape, lambda *_: (0,) * len(shape))


def upper_levels(field, before, after, velocity):
    tracers, levels, rows, width = field.shape
    block = (tracers, 1, rows, width)
    return pl.pallas_call(
        upper_kernel,
        grid=(levels - 1,),
        out_shape=jax.ShapeDtypeStruct(field.shape, jnp.float32),
        in_specs=[
            pl.BlockSpec(block, lambda level: (0, level + 1, 0, 0)),
            whole_spec(before.shape),
            whole_spec(after.shape),
            whole_spec(velocity.shape),
        ],
        out_specs=pl.BlockSpec(block, lambda level: (0, level + 1, 0, 0)),
        scratch_shapes=[pltpu.VMEM((4, 8, width), jnp.float32)],
        compiler_params=pltpu.CompilerParams(vmem_limit_bytes=VMEM_LIMIT),
        cost_estimate=SMALL_COST,
        name="upper_levels",
    )(field, before, after, velocity)


def surface_level(start, velocity, before_v, after_v, own1, own2, got1, got2, whole):
    tracers, _, rows, width = whole.shape
    values = (velocity, before_v, after_v, own1, own2, got1, got2)
    return pl.pallas_call(
        surface_kernel,
        grid=(1,),
        out_shape=jax.ShapeDtypeStruct(whole.shape, jnp.float32),
        in_specs=[pl.BlockSpec(memory_space=pltpu.SMEM)]
        + [whole_spec(v.shape) for v in values]
        + [pl.BlockSpec(memory_space=pl.ANY)],
        out_specs=pl.BlockSpec((tracers, 1, rows, width), lambda _: (0, 0, 0, 0)),
        input_output_aliases={len(values) + 1: 0},
        scratch_shapes=[pltpu.VMEM((4, 8, width), jnp.float32)],
        compiler_params=pltpu.CompilerParams(vmem_limit_bytes=VMEM_LIMIT),
        name="surface_level",
    )(start, *values, whole)


def per_device(
    tracer,
    velocity,
    coupling,
    sea_mask,
    send_rows,
    send_cols,
    intersection_near,
    intersection_slot,
    intersection_weight,
):
    field = tracer[0]
    speed = velocity[0]
    tracers, levels, rows, width = field.shape
    near, slot, weight = intersection_near[0], intersection_slot[0], intersection_weight[0]
    others = (0, 2, 3)
    before_v, after_v = edges(field, speed)
    before_v, lists = lax.optimization_barrier((before_v, (send_rows[0, 0], send_cols[0, 0])))
    packed = pack(field, *lists)
    before_v = moved(before_v, 1, False)
    pieces = [moved(packed[j], 1 - j, True) for j in range(len(packed))]
    after_v = moved(after_v, -1, False)
    partial = remap_near(1, near, slot, weight, pieces[1])
    pieces, before_v = lax.optimization_barrier(([pieces[j] for j in others], before_v))
    shared = (near, slot, weight, field, coupling[0], sea_mask[0], partial)
    odd = lax.axis_index("tile") & 1
    start1, start2 = (2 * odd).reshape(1), (2 - 2 * odd).reshape(1)
    own1 = remap(others, start1, pieces, *shared)
    got1 = swapped(own1, 1)
    pieces, own1 = lax.optimization_barrier((pieces, own1))
    own2 = remap(others, start2, pieces, *shared)
    got2 = swapped(own2, -1)
    before_v, got1 = lax.optimization_barrier((before_v, got1))
    whole = upper_levels(field, before_v, after_v, speed)
    return surface_level(start1, speed, before_v, after_v, own1, own2, got1, got2, whole)[None]


def solution(mesh):
    in_specs = (
        P("comp", None, None, "tile", None),
        P("comp", None, None, "tile", None),
        P("comp", None, "tile", None),
        P("comp", "tile", None),
        P("comp", "tile", None, None),
        P("comp", "tile", None, None),
        P("comp", None, "tile", None),
        P("comp", None, "tile", None),
        P("comp", None, "tile", None),
    )
    out_specs = P("comp", None, None, "tile", None)
    return jax.shard_map(
        per_device, mesh=mesh, in_specs=in_specs, out_specs=out_specs, check_vma=False
    )
```

```python
import functools

import jax
import jax.numpy as jnp
from jax import lax
from jax.experimental import pallas as pl
from jax.experimental.pallas import tpu as pltpu
from jax.sharding import PartitionSpec as P

diffusion = 0.12
LOW = 128
BLOCK = 1024
PACK_BLOCK = 512
VMEM_LIMIT = 48 * 2**20
FULL_VMEM = 60 * 2**20
SMALL_COST = pl.CostEstimate(flops=10**6, bytes_accessed=10**5, transcendentals=0)


def moved(value, steps, swap):
    tiles = lax.axis_size("tile")
    pairs = []
    for comp in range(lax.axis_size("comp")):
        for tile in range(tiles):
            target = (comp ^ 1 if swap else comp) * tiles + (tile + steps) % tiles
            pairs.append((comp * tiles + tile, target))
    return lax.ppermute(value, ("comp", "tile"), pairs)


def swapped(value, odd_step):
    tiles = lax.axis_size("tile")
    pairs = [(tile, (tile + (odd_step if tile % 2 else -odd_step)) % tiles) for tile in range(tiles)]
    return lax.ppermute(value, "tile", pairs)


def put_table(table, tracers, first, count, part):
    for high in range(count):
        value = part(high)
        leading = value.astype(jnp.bfloat16)
        rest = (value - leading.astype(jnp.float32)).astype(jnp.bfloat16)
        row = (first + high) * tracers
        table[row : row + tracers, :] = jnp.concatenate([leading, rest], axis=1)


def one_hot(low):
    width = low.shape[1]
    position = lax.broadcasted_iota(jnp.int32, (LOW, width), 0).astype(jnp.float32).astype(jnp.bfloat16)
    wanted = jnp.broadcast_to(low.astype(jnp.float32), (16, width)).astype(jnp.bfloat16)
    wanted = jnp.concatenate([wanted] * (LOW // 16), axis=0)
    return jnp.where(position == wanted, jnp.bfloat16(1), jnp.bfloat16(0))


def chosen(values, high):
    bit = 0
    while len(values) > 1:
        odd = ((high >> bit) & 1) == 1
        values = [jnp.where(odd, values[i + 1], values[i]) for i in range(0, len(values), 2)]
        bit += 1
    return values[0]


def low_product(table, entry, tracers):
    hot = one_hot(entry & (LOW - 1))
    hot = jnp.concatenate([hot, hot], axis=0)
    product = jnp.dot(table[...], hot, preferred_element_type=jnp.float32)
    return [product[at : at + tracers] for at in range(0, table.shape[0], tracers)]


def high_part(entry, tracers):
    return jnp.broadcast_to(entry // LOW, (tracers, entry.shape[1]))


def started(pairs, sems):
    copies = [pltpu.make_async_copy(source, target, sems.at[i]) for i, (source, target) in enumerate(pairs)]
    for copy in copies:
        copy.start()
    return copies


def edges_kernel(field, speed, before_v, after_v, upper, moving, sems):
    tracers, levels, grid_rows, _ = field.shape
    for copy in started(((speed, moving), (field.at[:, pl.ds(1, levels - 1)], upper)), sems):
        copy.wait()
    for which in range(2):
        for level in range(levels):
            at = (levels - 1) * tracers + which * levels + level
            after_v[at] = moving[which, level, :2]
            before_v[at] = moving[which, level, grid_rows - 2 :]

    for level in range(levels - 1):
        at = slice(level * tracers, (level + 1) * tracers)
        after_v[at] = upper[:, level, :2]
        before_v[at] = upper[:, level, grid_rows - 2 :]


def edges(field, speed):
    tracers, levels, grid_rows, width = field.shape
    edge = jax.ShapeDtypeStruct(((levels - 1) * tracers + 2 * levels, 2, width), jnp.float32)
    return pl.pallas_call(
        edges_kernel,
        in_specs=[pl.BlockSpec(memory_space=pltpu.HBM)] * 2,
        out_shape=[edge, edge],
        scratch_shapes=[
            pltpu.VMEM((tracers, levels - 1, grid_rows, width), jnp.float32),
            pltpu.VMEM(speed.shape, jnp.float32),
            pltpu.SemaphoreType.DMA((2,)),
        ],
        compiler_params=pltpu.CompilerParams(vmem_limit_bytes=FULL_VMEM),
        cost_estimate=SMALL_COST,
        name="edges",
    )(field, speed)


def pack_kernel(field, rows, cols, *rest):
    outs, table = rest[:-1], rest[-1]
    tracers, _, grid_rows, width = field.shape
    per_row = width // LOW

    def part(high):
        low = high % per_row * LOW
        return field[:, 0, high // per_row, low : low + LOW]

    put_table(table, tracers, 0, grid_rows * per_row, part)
    for near in range(rows.shape[0]):
        for start in range(0, rows.shape[1], PACK_BLOCK):
            at = slice(start, start + PACK_BLOCK)
            entry = rows[near : near + 1, at] * width + cols[near : near + 1, at]
            product = low_product(table, entry, tracers)
            outs[near][:, at] = chosen(product, high_part(entry, tracers))


def level_spec(field):
    tracers, _, rows, width = field.shape
    return pl.BlockSpec((tracers, 1, rows, width), lambda *_: (0, 0, 0, 0))


def pack(field, rows, cols):
    tracers, _, grid_rows, width = field.shape
    neighbours, capacity = rows.shape
    piece = jax.ShapeDtypeStruct((tracers, capacity), jnp.float32)
    return pl.pallas_call(
        pack_kernel,
        grid=(1,),
        in_specs=[level_spec(field), whole_spec(rows.shape), whole_spec(cols.shape)],
        out_specs=[whole_spec(piece.shape)] * neighbours,
        out_shape=[piece] * neighbours,
        scratch_shapes=[pltpu.VMEM((grid_rows * width // LOW * tracers, 2 * LOW), jnp.bfloat16)],
        compiler_params=pltpu.CompilerParams(vmem_limit_bytes=VMEM_LIMIT),
        cost_estimate=SMALL_COST,
        name="pack",
    )(field, rows, cols)


def added_reads(sources, near, slot, weight, table, tracers, row, at):
    total = None
    for k in range(near.shape[0]):
        which = near[k, pl.ds(row, 1), at]
        entry = slot[k, pl.ds(row, 1), at]
        product = low_product(table, entry, tracers)
        high = high_part(entry, tracers)
        count = len(product) // len(sources)
        wide = jnp.broadcast_to(which, high.shape)
        read = chosen(product[:count], high)
        inside = which == sources[0]
        for rank in range(1, len(sources)):
            part = chosen(product[rank * count : (rank + 1) * count], high)
            read = jnp.where(wide == sources[rank], part, read)
            inside = inside | (which == sources[rank])
        term = jnp.where(inside, weight[k, pl.ds(row, 1), at], 0.0) * read
        total = term if total is None else total + term
    return total


def put_pieces(table, pieces):
    tracers, capacity = pieces[0].shape
    count = capacity // LOW
    for index, piece in enumerate(pieces):
        put_table(
            table, tracers, index * count, count, lambda high, piece=piece: piece[:, high * LOW : (high + 1) * LOW]
        )


def near_kernel(sources, near, slot, weight, piece, out, table):
    tracers = piece.shape[0]
    put_pieces(table, [piece])
    width = near.shape[2]
    for row in range(near.shape[1]):

        def body(step, carry, row=row):
            at = pl.ds(pl.multiple_of(step * BLOCK, BLOCK), BLOCK)
            out[:, row, at] = added_reads(sources, near, slot, weight, table, tracers, row, at)
            return carry

        lax.fori_loop(0, width // BLOCK, body, 0)


def remap_near(source, near, slot, weight, piece):
    tracers, capacity = piece.shape
    _, rows, width = near.shape
    return pl.pallas_call(
        functools.partial(near_kernel, (source,)),
        out_shape=jax.ShapeDtypeStruct((tracers, rows, width), jnp.float32),
        scratch_shapes=[pltpu.VMEM((capacity // LOW * tracers, 2 * LOW), jnp.bfloat16)],
        compiler_params=pltpu.CompilerParams(vmem_limit_bytes=VMEM_LIMIT),
        cost_estimate=SMALL_COST,
        name="remap_near",
    )(near, slot, weight, piece)


def remap_kernel(sources, start, near, slot, weight, field, coupling, mask, partial, *rest):
    pieces, (out, table) = rest[:-2], rest[-2:]
    tracers = field.shape[0]
    put_pieces(table, pieces)
    for place in range(out.shape[1]):
        row = start[0] + place

        def body(step, carry, place=place, row=row):
            at = pl.ds(pl.multiple_of(step * BLOCK, BLOCK), BLOCK)
            total = added_reads(sources, near, slot, weight, table, tracers, row, at)
            total = total + partial[:, row, at]
            own = field[:, 0, row, at]
            wet = mask[pl.ds(row, 1), at].astype(jnp.float32)
            out[:, place, at] = own + coupling[:, row, at] * wet * (total - own)
            return carry

        lax.fori_loop(0, field.shape[3] // BLOCK, body, 0)


def remap(sources, start, pieces, near, slot, weight, field, coupling, mask, partial):
    tracers, capacity = pieces[0].shape
    out = (tracers, 2, field.shape[3])
    specs = [whole_spec(v.shape) for v in (near, slot, weight, coupling, mask, partial, *pieces)]
    specs.insert(3, level_spec(field))
    specs.insert(0, pl.BlockSpec(memory_space=pltpu.SMEM))
    return pl.pallas_call(
        functools.partial(remap_kernel, sources),
        grid=(1,),
        in_specs=specs,
        out_specs=whole_spec(out),
        out_shape=jax.ShapeDtypeStruct(out, jnp.float32),
        scratch_shapes=[pltpu.VMEM((len(pieces) * capacity // LOW * tracers, 2 * LOW), jnp.bfloat16)],
        compiler_params=pltpu.CompilerParams(vmem_limit_bytes=VMEM_LIMIT),
        cost_estimate=pl.CostEstimate(flops=15 * 10**9, bytes_accessed=10**6, transcendentals=0),
        name="remap",
    )(start, near, slot, weight, field, coupling, mask, partial, *pieces)


def substep(west, field, east, speed_x, speed_y):
    width = field.shape[1]
    north = pltpu.roll(field, width - 1, axis=1)
    south = pltpu.roll(field, 1, axis=1)
    return (
        (1 - 4 * diffusion) * field
        + ((diffusion - 0.5 * speed_x) * east + (diffusion + 0.5 * speed_x) * west)
        + ((diffusion - 0.5 * speed_y) * north + (diffusion + 0.5 * speed_y) * south)
    )


def transported(rows, speeds):
    for _ in range(2):
        rows = [substep(*rows[i - 1 : i + 2], *speeds[i - 1]) for i in range(1, len(rows) - 1)]
        speeds = speeds[1:-1]
    return rows


def speed_rows(velocity, before_v, after_v, level, tracers):
    levels, grid_rows = velocity.shape[1:3]
    pairs = []
    for row in range(-1, grid_rows + 1):
        pair = []
        for which in range(2):
            at = (levels - 1) * tracers + which * levels + level
            if row < 0:
                pair.append(before_v[at, 1:])
            elif row < grid_rows:
                pair.append(velocity[which, level, row : row + 1])
            else:
                pair.append(after_v[at, :1])
        pairs.append(pair)
    return pairs


def upper_kernel(field, before_v, after_v, velocity, out):
    level = pl.program_id(0)
    tracers, _, grid_rows, _ = field.shape
    at = pl.ds(level * tracers, tracers)
    rows = [before_v[at, row] for row in range(2)]
    rows += [field[:, 0, row] for row in range(grid_rows)]
    rows += [after_v[at, row] for row in range(2)]
    speeds = speed_rows(velocity, before_v, after_v, level + 1, tracers)
    for row, value in enumerate(transported(rows, speeds)):
        out[:, 0, row] = value


def surface_kernel(start, velocity, before_v, after_v, own1, own2, got1, got2, whole, out):
    del whole
    odd = start[0] > 0
    first, last = [], []
    before, after = [], []
    for row in range(2):
        one, two = own1[:, row], own2[:, row]
        far1, far2 = got1[:, row], got2[:, row]
        first.append(jnp.where(odd, two, one))
        last.append(jnp.where(odd, one, two))
        before.append(jnp.where(odd, far2, far1))
        after.append(jnp.where(odd, far1, far2))
    speeds = speed_rows(velocity, before_v, after_v, 0, own1.shape[0])
    for row, value in enumerate(transported(before + first + last + after, speeds)):
        out[:, 0, row] = value


def whole_spec(shape):
    return pl.BlockSpec(shape, lambda *_: (0,) * len(shape))


def upper_levels(field, before, after, velocity):
    tracers, levels, rows, width = field.shape
    block = (tracers, 1, rows, width)
    return pl.pallas_call(
        upper_kernel,
        grid=(levels - 1,),
        out_shape=jax.ShapeDtypeStruct(field.shape, jnp.float32),
        in_specs=[
            pl.BlockSpec(block, lambda level: (0, level + 1, 0, 0)),
            whole_spec(before.shape),
            whole_spec(after.shape),
            whole_spec(velocity.shape),
        ],
        out_specs=pl.BlockSpec(block, lambda level: (0, level + 1, 0, 0)),
        compiler_params=pltpu.CompilerParams(vmem_limit_bytes=VMEM_LIMIT),
        cost_estimate=SMALL_COST,
        name="upper_levels",
    )(field, before, after, velocity)


def surface_level(start, velocity, before_v, after_v, own1, own2, got1, got2, whole):
    tracers, _, rows, width = whole.shape
    values = (velocity, before_v, after_v, own1, own2, got1, got2)
    return pl.pallas_call(
        surface_kernel,
        grid=(1,),
        out_shape=jax.ShapeDtypeStruct(whole.shape, jnp.float32),
        in_specs=[pl.BlockSpec(memory_space=pltpu.SMEM)]
        + [whole_spec(v.shape) for v in values]
        + [pl.BlockSpec(memory_space=pl.ANY)],
        out_specs=pl.BlockSpec((tracers, 1, rows, width), lambda _: (0, 0, 0, 0)),
        input_output_aliases={len(values) + 1: 0},
        compiler_params=pltpu.CompilerParams(vmem_limit_bytes=VMEM_LIMIT),
        name="surface_level",
    )(start, *values, whole)


def per_device(
    tracer,
    velocity,
    coupling,
    sea_mask,
    send_rows,
    send_cols,
    intersection_near,
    intersection_slot,
    intersection_weight,
):
    field = tracer[0]
    speed = velocity[0]
    tracers, levels, rows, width = field.shape
    near, slot, weight = intersection_near[0], intersection_slot[0], intersection_weight[0]
    others = (0, 2, 3)
    before_v, after_v = edges(field, speed)
    before_v, lists = lax.optimization_barrier((before_v, (send_rows[0, 0], send_cols[0, 0])))
    packed = pack(field, *lists)
    before_v = moved(before_v, 1, False)
    pieces = [moved(packed[j], 1 - j, True) for j in range(len(packed))]
    after_v = moved(after_v, -1, False)
    partial = remap_near(1, near, slot, weight, pieces[1])
    pieces, before_v = lax.optimization_barrier(([pieces[j] for j in others], before_v))
    shared = (near, slot, weight, field, coupling[0], sea_mask[0], partial)
    odd = lax.axis_index("tile") & 1
    start1, start2 = (2 * odd).reshape(1), (2 - 2 * odd).reshape(1)
    own1 = remap(others, start1, pieces, *shared)
    got1 = swapped(own1, 1)
    pieces, own1 = lax.optimization_barrier((pieces, own1))
    own2 = remap(others, start2, pieces, *shared)
    got2 = swapped(own2, -1)
    before_v, got1 = lax.optimization_barrier((before_v, got1))
    whole = upper_levels(field, before_v, after_v, speed)
    return surface_level(start1, speed, before_v, after_v, own1, own2, got1, got2, whole)[None]


def solution(mesh):
    in_specs = (
        P("comp", None, None, "tile", None),
        P("comp", None, None, "tile", None),
        P("comp", None, "tile", None),
        P("comp", "tile", None),
        P("comp", "tile", None, None),
        P("comp", "tile", None, None),
        P("comp", None, "tile", None),
        P("comp", None, "tile", None),
        P("comp", None, "tile", None),
    )
    out_specs = P("comp", None, None, "tile", None)
    return jax.shard_map(
        per_device, mesh=mesh, in_specs=in_specs, out_specs=out_specs, check_vma=False
    )
```

```python
import functools

import jax
import jax.numpy as jnp
from jax import lax
from jax.experimental import pallas as pl
from jax.experimental.pallas import tpu as pltpu
from jax.sharding import PartitionSpec as P

diffusion = 0.12
LOW = 128
BLOCK = 1024
LANE_TERMS = (0, 1)
PACK_BLOCK = 512
VMEM_LIMIT = 48 * 2**20
FULL_VMEM = 60 * 2**20
SMALL_COST = pl.CostEstimate(flops=10**6, bytes_accessed=10**5, transcendentals=0)


def moved(value, steps, swap):
    tiles = lax.axis_size("tile")
    pairs = []
    for comp in range(lax.axis_size("comp")):
        for tile in range(tiles):
            target = (comp ^ 1 if swap else comp) * tiles + (tile + steps) % tiles
            pairs.append((comp * tiles + tile, target))
    return lax.ppermute(value, ("comp", "tile"), pairs)


def swapped(value, odd_step):
    tiles = lax.axis_size("tile")
    pairs = [(tile, (tile + (odd_step if tile % 2 else -odd_step)) % tiles) for tile in range(tiles)]
    return lax.ppermute(value, "tile", pairs)


def put_table(table, tracers, first, count, part):
    for high in range(count):
        value = part(high)
        leading = value.astype(jnp.bfloat16)
        rest = (value - leading.astype(jnp.float32)).astype(jnp.bfloat16)
        row = (first + high) * tracers
        table[row : row + tracers, :] = jnp.concatenate([leading, rest], axis=1)


def one_hot(low):
    width = low.shape[1]
    position = lax.broadcasted_iota(jnp.int32, (LOW, width), 0).astype(jnp.float32).astype(jnp.bfloat16)
    wanted = jnp.broadcast_to(low.astype(jnp.float32), (16, width)).astype(jnp.bfloat16)
    wanted = jnp.concatenate([wanted] * (LOW // 16), axis=0)
    return jnp.where(position == wanted, jnp.bfloat16(1), jnp.bfloat16(0))


def chosen(values, high):
    bit = 0
    while len(values) > 1:
        odd = ((high >> bit) & 1) == 1
        values = [jnp.where(odd, values[i + 1], values[i]) for i in range(0, len(values), 2)]
        bit += 1
    return values[0]


def low_product(table, entry, tracers):
    hot = one_hot(entry & (LOW - 1))
    hot = jnp.concatenate([hot, hot], axis=0)
    product = jnp.dot(table[...], hot, preferred_element_type=jnp.float32)
    return [product[at : at + tracers] for at in range(0, table.shape[0], tracers)]


def high_part(entry, tracers):
    return jnp.broadcast_to(entry // LOW, (tracers, entry.shape[1]))


def started(pairs, sems):
    copies = [pltpu.make_async_copy(source, target, sems.at[i]) for i, (source, target) in enumerate(pairs)]
    for copy in copies:
        copy.start()
    return copies


def edges_kernel(field, speed, before_v, after_v, upper, moving, sems):
    tracers, levels, grid_rows, _ = field.shape
    for copy in started(((speed, moving), (field.at[:, pl.ds(1, levels - 1)], upper)), sems):
        copy.wait()
    for which in range(2):
        for level in range(levels):
            at = (levels - 1) * tracers + which * levels + level
            after_v[at] = moving[which, level, :2]
            before_v[at] = moving[which, level, grid_rows - 2 :]

    for level in range(levels - 1):
        at = slice(level * tracers, (level + 1) * tracers)
        after_v[at] = upper[:, level, :2]
        before_v[at] = upper[:, level, grid_rows - 2 :]


def edges(field, speed):
    tracers, levels, grid_rows, width = field.shape
    edge = jax.ShapeDtypeStruct(((levels - 1) * tracers + 2 * levels, 2, width), jnp.float32)
    return pl.pallas_call(
        edges_kernel,
        in_specs=[pl.BlockSpec(memory_space=pltpu.HBM)] * 2,
        out_shape=[edge, edge],
        scratch_shapes=[
            pltpu.VMEM((tracers, levels - 1, grid_rows, width), jnp.float32),
            pltpu.VMEM(speed.shape, jnp.float32),
            pltpu.SemaphoreType.DMA((2,)),
        ],
        compiler_params=pltpu.CompilerParams(vmem_limit_bytes=FULL_VMEM),
        cost_estimate=SMALL_COST,
        name="edges",
    )(field, speed)


def pack_kernel(field, rows, cols, *rest):
    outs, table = rest[:-1], rest[-1]
    tracers, _, grid_rows, width = field.shape
    per_row = width // LOW

    def part(high):
        low = high % per_row * LOW
        return field[:, 0, high // per_row, low : low + LOW]

    put_table(table, tracers, 0, grid_rows * per_row, part)
    for near in range(rows.shape[0]):
        for start in range(0, rows.shape[1], PACK_BLOCK):
            at = slice(start, start + PACK_BLOCK)
            entry = rows[near : near + 1, at] * width + cols[near : near + 1, at]
            product = low_product(table, entry, tracers)
            outs[near][:, at] = chosen(product, high_part(entry, tracers))


def level_spec(field):
    tracers, _, rows, width = field.shape
    return pl.BlockSpec((tracers, 1, rows, width), lambda *_: (0, 0, 0, 0))


def pack(field, rows, cols):
    tracers, _, grid_rows, width = field.shape
    neighbours, capacity = rows.shape
    piece = jax.ShapeDtypeStruct((tracers, capacity), jnp.float32)
    return pl.pallas_call(
        pack_kernel,
        grid=(1,),
        in_specs=[level_spec(field), whole_spec(rows.shape), whole_spec(cols.shape)],
        out_specs=[whole_spec(piece.shape)] * neighbours,
        out_shape=[piece] * neighbours,
        scratch_shapes=[pltpu.VMEM((grid_rows * width // LOW * tracers, 2 * LOW), jnp.bfloat16)],
        compiler_params=pltpu.CompilerParams(vmem_limit_bytes=VMEM_LIMIT),
        cost_estimate=SMALL_COST,
        name="pack",
    )(field, rows, cols)


def lane_chosen(piece, low, bits, rows, first, level):
    if level == 0:
        part = piece[rows, first * LOW : (first + 1) * LOW]
        return jnp.take_along_axis(part, low, axis=1, mode="promise_in_bounds")
    half = 1 << (level - 1)
    even = lane_chosen(piece, low, bits, rows, first, level - 1)
    odd = lane_chosen(piece, low, bits, rows, first + half, level - 1)
    return jnp.where(bits[level - 1], odd, even)


def lane_reads(sources, pieces, which, entry):
    tracers, capacity = pieces[0].shape
    low = jnp.broadcast_to(entry & (LOW - 1), (8, LOW))
    high = jnp.broadcast_to(entry // LOW, (8, LOW))
    wide = jnp.broadcast_to(which, (8, LOW))
    depth = (capacity // LOW).bit_length() - 1
    bits = [((high >> bit) & 1) == 1 for bit in range(depth)]
    halves = []
    for at in range(0, tracers, 8):
        read = None
        for source, piece in zip(sources, pieces):
            part = lane_chosen(piece, low, bits, slice(at, at + 8), 0, depth)
            read = part if read is None else jnp.where(wide == source, part, read)
        halves.append(read)
    return jnp.concatenate(halves, axis=0)


def product_reads(sources, table, which, entry, tracers):
    product = low_product(table, entry, tracers)
    high = high_part(entry, tracers)
    count = len(product) // len(sources)
    wide = jnp.broadcast_to(which, high.shape)
    read = None
    for rank, source in enumerate(sources):
        part = chosen(product[rank * count : (rank + 1) * count], high)
        read = part if read is None else jnp.where(wide == source, part, read)
    return read


def added_reads(sources, pieces, near, slot, weight, table, tracers, row, col):
    lane_terms = {k: [] for k in LANE_TERMS}
    lane_work = [(k, at) for k in LANE_TERMS for at in range(0, BLOCK, LOW)]
    products = [k for k in range(near.shape[0]) if k not in LANE_TERMS]
    total = None

    lists = [[v[k, pl.ds(row, 1), pl.ds(col, BLOCK)] for v in (near, slot, weight)] for k in range(near.shape[0])]
    for item in lists:
        inside = item[0] == sources[0]
        for source in sources[1:]:
            inside = inside | (item[0] == source)
        item[2] = jnp.where(inside, item[2], 0.0)

    for place, k in enumerate(products):
        which, entry, share = lists[k]
        term = share * product_reads(sources, table, which, entry, tracers)
        total = term if total is None else total + term
        begin, end = (len(lane_work) * p // len(products) for p in (place, place + 1))
        for lane_k, start in lane_work[begin:end]:
            which, entry, share = (v[:, start : start + LOW] for v in lists[lane_k])
            lane_terms[lane_k].append(share * lane_reads(sources, pieces, which, entry))
    for parts in lane_terms.values():
        total = total + jnp.concatenate(parts, axis=1)
    return total


def put_pieces(table, pieces):
    tracers, capacity = pieces[0].shape
    count = capacity // LOW
    for index, piece in enumerate(pieces):
        put_table(
            table, tracers, index * count, count, lambda high, piece=piece: piece[:, high * LOW : (high + 1) * LOW]
        )


def near_kernel(sources, near, slot, weight, piece, out, table):
    tracers = piece.shape[0]
    put_pieces(table, [piece])
    width = near.shape[2]
    for row in range(near.shape[1]):

        def body(step, carry, row=row):
            col = pl.multiple_of(step * BLOCK, BLOCK)
            out[:, row, pl.ds(col, BLOCK)] = added_reads(
                sources, [piece], near, slot, weight, table, tracers, row, col
            )
            return carry

        lax.fori_loop(0, width // BLOCK, body, 0)


def remap_near(source, near, slot, weight, piece):
    tracers, capacity = piece.shape
    _, rows, width = near.shape
    return pl.pallas_call(
        functools.partial(near_kernel, (source,)),
        out_shape=jax.ShapeDtypeStruct((tracers, rows, width), jnp.float32),
        scratch_shapes=[pltpu.VMEM((capacity // LOW * tracers, 2 * LOW), jnp.bfloat16)],
        compiler_params=pltpu.CompilerParams(vmem_limit_bytes=VMEM_LIMIT),
        cost_estimate=SMALL_COST,
        name="remap_near",
    )(near, slot, weight, piece)


def remap_kernel(sources, start, near, slot, weight, field, coupling, mask, partial, *rest):
    pieces, (out, table) = rest[:-2], rest[-2:]
    tracers = field.shape[0]
    put_pieces(table, pieces)
    for place in range(out.shape[1]):
        row = start[0] + place

        def body(step, carry, place=place, row=row):
            col = pl.multiple_of(step * BLOCK, BLOCK)
            at = pl.ds(col, BLOCK)
            total = added_reads(sources, pieces, near, slot, weight, table, tracers, row, col)
            total = total + partial[:, row, at]
            own = field[:, 0, row, at]
            wet = mask[pl.ds(row, 1), at].astype(jnp.float32)
            out[:, place, at] = own + coupling[:, row, at] * wet * (total - own)
            return carry

        lax.fori_loop(0, field.shape[3] // BLOCK, body, 0)


def remap(sources, start, pieces, near, slot, weight, field, coupling, mask, partial):
    tracers, capacity = pieces[0].shape
    out = (tracers, 2, field.shape[3])
    specs = [whole_spec(v.shape) for v in (near, slot, weight, coupling, mask, partial, *pieces)]
    specs.insert(3, level_spec(field))
    specs.insert(0, pl.BlockSpec(memory_space=pltpu.SMEM))
    return pl.pallas_call(
        functools.partial(remap_kernel, sources),
        grid=(1,),
        in_specs=specs,
        out_specs=whole_spec(out),
        out_shape=jax.ShapeDtypeStruct(out, jnp.float32),
        scratch_shapes=[pltpu.VMEM((len(pieces) * capacity // LOW * tracers, 2 * LOW), jnp.bfloat16)],
        compiler_params=pltpu.CompilerParams(vmem_limit_bytes=VMEM_LIMIT),
        cost_estimate=pl.CostEstimate(flops=15 * 10**9, bytes_accessed=10**6, transcendentals=0),
        name="remap",
    )(start, near, slot, weight, field, coupling, mask, partial, *pieces)


def substep(west, field, east, speed_x, speed_y):
    width = field.shape[1]
    north = pltpu.roll(field, width - 1, axis=1)
    south = pltpu.roll(field, 1, axis=1)
    return (
        (1 - 4 * diffusion) * field
        + ((diffusion - 0.5 * speed_x) * east + (diffusion + 0.5 * speed_x) * west)
        + ((diffusion - 0.5 * speed_y) * north + (diffusion + 0.5 * speed_y) * south)
    )


def transported(rows, speeds):
    for _ in range(2):
        rows = [substep(*rows[i - 1 : i + 2], *speeds[i - 1]) for i in range(1, len(rows) - 1)]
        speeds = speeds[1:-1]
    return rows


def speed_rows(velocity, before_v, after_v, level, tracers):
    levels, grid_rows = velocity.shape[1:3]
    pairs = []
    for row in range(-1, grid_rows + 1):
        pair = []
        for which in range(2):
            at = (levels - 1) * tracers + which * levels + level
            if row < 0:
                pair.append(before_v[at, 1:])
            elif row < grid_rows:
                pair.append(velocity[which, level, row : row + 1])
            else:
                pair.append(after_v[at, :1])
        pairs.append(pair)
    return pairs


def upper_kernel(field, before_v, after_v, velocity, out):
    level = pl.program_id(0)
    tracers, _, grid_rows, _ = field.shape
    at = pl.ds(level * tracers, tracers)
    rows = [before_v[at, row] for row in range(2)]
    rows += [field[:, 0, row] for row in range(grid_rows)]
    rows += [after_v[at, row] for row in range(2)]
    speeds = speed_rows(velocity, before_v, after_v, level + 1, tracers)
    for row, value in enumerate(transported(rows, speeds)):
        out[:, 0, row] = value


def surface_kernel(start, velocity, before_v, after_v, own1, own2, got1, got2, whole, out):
    del whole
    odd = start[0] > 0
    first, last = [], []
    before, after = [], []
    for row in range(2):
        one, two = own1[:, row], own2[:, row]
        far1, far2 = got1[:, row], got2[:, row]
        first.append(jnp.where(odd, two, one))
        last.append(jnp.where(odd, one, two))
        before.append(jnp.where(odd, far2, far1))
        after.append(jnp.where(odd, far1, far2))
    speeds = speed_rows(velocity, before_v, after_v, 0, own1.shape[0])
    for row, value in enumerate(transported(before + first + last + after, speeds)):
        out[:, 0, row] = value


def whole_spec(shape):
    return pl.BlockSpec(shape, lambda *_: (0,) * len(shape))


def upper_levels(field, before, after, velocity):
    tracers, levels, rows, width = field.shape
    block = (tracers, 1, rows, width)
    return pl.pallas_call(
        upper_kernel,
        grid=(levels - 1,),
        out_shape=jax.ShapeDtypeStruct(field.shape, jnp.float32),
        in_specs=[
            pl.BlockSpec(block, lambda level: (0, level + 1, 0, 0)),
            whole_spec(before.shape),
            whole_spec(after.shape),
            whole_spec(velocity.shape),
        ],
        out_specs=pl.BlockSpec(block, lambda level: (0, level + 1, 0, 0)),
        compiler_params=pltpu.CompilerParams(vmem_limit_bytes=VMEM_LIMIT),
        cost_estimate=SMALL_COST,
        name="upper_levels",
    )(field, before, after, velocity)


def surface_level(start, velocity, before_v, after_v, own1, own2, got1, got2, whole):
    tracers, _, rows, width = whole.shape
    values = (velocity, before_v, after_v, own1, own2, got1, got2)
    return pl.pallas_call(
        surface_kernel,
        grid=(1,),
        out_shape=jax.ShapeDtypeStruct(whole.shape, jnp.float32),
        in_specs=[pl.BlockSpec(memory_space=pltpu.SMEM)]
        + [whole_spec(v.shape) for v in values]
        + [pl.BlockSpec(memory_space=pl.ANY)],
        out_specs=pl.BlockSpec((tracers, 1, rows, width), lambda _: (0, 0, 0, 0)),
        input_output_aliases={len(values) + 1: 0},
        compiler_params=pltpu.CompilerParams(vmem_limit_bytes=VMEM_LIMIT),
        name="surface_level",
    )(start, *values, whole)


def per_device(
    tracer,
    velocity,
    coupling,
    sea_mask,
    send_rows,
    send_cols,
    intersection_near,
    intersection_slot,
    intersection_weight,
):
    field = tracer[0]
    speed = velocity[0]
    tracers, levels, rows, width = field.shape
    near, slot, weight = intersection_near[0], intersection_slot[0], intersection_weight[0]
    others = (0, 2, 3)
    before_v, after_v = edges(field, speed)
    before_v, lists = lax.optimization_barrier((before_v, (send_rows[0, 0], send_cols[0, 0])))
    packed = pack(field, *lists)
    before_v = moved(before_v, 1, False)
    pieces = [moved(packed[j], 1 - j, True) for j in range(len(packed))]
    after_v = moved(after_v, -1, False)
    partial = remap_near(1, near, slot, weight, pieces[1])
    pieces, before_v = lax.optimization_barrier(([pieces[j] for j in others], before_v))
    shared = (near, slot, weight, field, coupling[0], sea_mask[0], partial)
    odd = lax.axis_index("tile") & 1
    start1, start2 = (2 * odd).reshape(1), (2 - 2 * odd).reshape(1)
    own1 = remap(others, start1, pieces, *shared)
    got1 = swapped(own1, 1)
    pieces, own1 = lax.optimization_barrier((pieces, own1))
    own2 = remap(others, start2, pieces, *shared)
    got2 = swapped(own2, -1)
    before_v, got1 = lax.optimization_barrier((before_v, got1))
    whole = upper_levels(field, before_v, after_v, speed)
    return surface_level(start1, speed, before_v, after_v, own1, own2, got1, got2, whole)[None]


def solution(mesh):
    in_specs = (
        P("comp", None, None, "tile", None),
        P("comp", None, None, "tile", None),
        P("comp", None, "tile", None),
        P("comp", "tile", None),
        P("comp", "tile", None, None),
        P("comp", "tile", None, None),
        P("comp", None, "tile", None),
        P("comp", None, "tile", None),
        P("comp", None, "tile", None),
    )
    out_specs = P("comp", None, None, "tile", None)
    return jax.shard_map(
        per_device, mesh=mesh, in_specs=in_specs, out_specs=out_specs, check_vma=False
    )
```

```python
import functools

import jax
import jax.numpy as jnp
from jax import lax
from jax.experimental import pallas as pl
from jax.experimental.pallas import tpu as pltpu
from jax.sharding import PartitionSpec as P

diffusion = 0.12
LOW = 128
BLOCK = 1024
LANE_TERMS = (0, 1)
PACK_BLOCK = 512
VMEM_LIMIT = 48 * 2**20
FULL_VMEM = 60 * 2**20
SMALL_COST = pl.CostEstimate(flops=10**6, bytes_accessed=10**5, transcendentals=0)


def moved(value, steps, swap):
    tiles = lax.axis_size("tile")
    pairs = []
    for comp in range(lax.axis_size("comp")):
        for tile in range(tiles):
            target = (comp ^ 1 if swap else comp) * tiles + (tile + steps) % tiles
            pairs.append((comp * tiles + tile, target))
    return lax.ppermute(value, ("comp", "tile"), pairs)


def swapped(value, odd_step):
    tiles = lax.axis_size("tile")
    pairs = [(tile, (tile + (odd_step if tile % 2 else -odd_step)) % tiles) for tile in range(tiles)]
    return lax.ppermute(value, "tile", pairs)


def put_table(table, tracers, first, count, part):
    for high in range(count):
        value = part(high)
        leading = value.astype(jnp.bfloat16)
        rest = (value - leading.astype(jnp.float32)).astype(jnp.bfloat16)
        row = (first + high) * tracers
        table[row : row + tracers, :] = jnp.concatenate([leading, rest], axis=1)


def one_hot(low):
    width = low.shape[1]
    position = lax.broadcasted_iota(jnp.int32, (LOW, width), 0).astype(jnp.float32).astype(jnp.bfloat16)
    wanted = jnp.broadcast_to(low.astype(jnp.float32), (16, width)).astype(jnp.bfloat16)
    wanted = jnp.concatenate([wanted] * (LOW // 16), axis=0)
    return jnp.where(position == wanted, jnp.bfloat16(1), jnp.bfloat16(0))


def chosen(values, high):
    bit = 0
    while len(values) > 1:
        odd = ((high >> bit) & 1) == 1
        values = [jnp.where(odd, values[i + 1], values[i]) for i in range(0, len(values), 2)]
        bit += 1
    return values[0]


def low_product(table, entry, tracers):
    hot = one_hot(entry & (LOW - 1))
    hot = jnp.concatenate([hot, hot], axis=0)
    product = jnp.dot(table[...], hot, preferred_element_type=jnp.float32)
    return [product[at : at + tracers] for at in range(0, table.shape[0], tracers)]


def high_part(entry, tracers):
    return jnp.broadcast_to(entry // LOW, (tracers, entry.shape[1]))


def started(pairs, sems):
    copies = [pltpu.make_async_copy(source, target, sems.at[i]) for i, (source, target) in enumerate(pairs)]
    for copy in copies:
        copy.start()
    return copies


def edges_kernel(field, speed, before_v, after_v, upper, moving, sems):
    tracers, levels, grid_rows, _ = field.shape
    for copy in started(((speed, moving), (field.at[:, pl.ds(1, levels - 1)], upper)), sems):
        copy.wait()
    for which in range(2):
        for level in range(levels):
            at = (levels - 1) * tracers + which * levels + level
            after_v[at] = moving[which, level, :2]
            before_v[at] = moving[which, level, grid_rows - 2 :]

    for level in range(levels - 1):
        at = slice(level * tracers, (level + 1) * tracers)
        after_v[at] = upper[:, level, :2]
        before_v[at] = upper[:, level, grid_rows - 2 :]


def edges(field, speed):
    tracers, levels, grid_rows, width = field.shape
    edge = jax.ShapeDtypeStruct(((levels - 1) * tracers + 2 * levels, 2, width), jnp.float32)
    return pl.pallas_call(
        edges_kernel,
        in_specs=[pl.BlockSpec(memory_space=pltpu.HBM)] * 2,
        out_shape=[edge, edge],
        scratch_shapes=[
            pltpu.VMEM((tracers, levels - 1, grid_rows, width), jnp.float32),
            pltpu.VMEM(speed.shape, jnp.float32),
            pltpu.SemaphoreType.DMA((2,)),
        ],
        compiler_params=pltpu.CompilerParams(vmem_limit_bytes=FULL_VMEM),
        cost_estimate=SMALL_COST,
        name="edges",
    )(field, speed)


def pack_kernel(field, rows, cols, *rest):
    outs, table = rest[:-1], rest[-1]
    tracers, _, grid_rows, width = field.shape
    per_row = width // LOW

    def part(high):
        low = high % per_row * LOW
        return field[:, 0, high // per_row, low : low + LOW]

    put_table(table, tracers, 0, grid_rows * per_row, part)
    for near in range(rows.shape[0]):
        for start in range(0, rows.shape[1], PACK_BLOCK):
            at = slice(start, start + PACK_BLOCK)
            entry = rows[near : near + 1, at] * width + cols[near : near + 1, at]
            product = low_product(table, entry, tracers)
            outs[near][:, at] = chosen(product, high_part(entry, tracers))


def level_spec(field):
    tracers, _, rows, width = field.shape
    return pl.BlockSpec((tracers, 1, rows, width), lambda *_: (0, 0, 0, 0))


def pack(field, rows, cols):
    tracers, _, grid_rows, width = field.shape
    neighbours, capacity = rows.shape
    piece = jax.ShapeDtypeStruct((tracers, capacity), jnp.float32)
    return pl.pallas_call(
        pack_kernel,
        grid=(1,),
        in_specs=[level_spec(field), whole_spec(rows.shape), whole_spec(cols.shape)],
        out_specs=[whole_spec(piece.shape)] * neighbours,
        out_shape=[piece] * neighbours,
        scratch_shapes=[pltpu.VMEM((grid_rows * width // LOW * tracers, 2 * LOW), jnp.bfloat16)],
        compiler_params=pltpu.CompilerParams(vmem_limit_bytes=VMEM_LIMIT),
        cost_estimate=SMALL_COST,
        name="pack",
    )(field, rows, cols)


def lane_chosen(piece, low, bits, rows, first, level):
    if level == 0:
        part = piece[rows, first * LOW : (first + 1) * LOW]
        return jnp.take_along_axis(part, low, axis=1, mode="promise_in_bounds")
    half = 1 << (level - 1)
    even = lane_chosen(piece, low, bits, rows, first, level - 1)
    odd = lane_chosen(piece, low, bits, rows, first + half, level - 1)
    return jnp.where(bits[level - 1], odd, even)


def lane_reads(sources, pieces, which, entry):
    tracers, capacity = pieces[0].shape
    low = jnp.broadcast_to(entry & (LOW - 1), (8, LOW))
    high = jnp.broadcast_to(entry // LOW, (8, LOW))
    wide = jnp.broadcast_to(which, (8, LOW))
    depth = (capacity // LOW).bit_length() - 1
    bits = [((high >> bit) & 1) == 1 for bit in range(depth)]
    halves = []
    for at in range(0, tracers, 8):
        read = None
        for source, piece in zip(sources, pieces):
            part = lane_chosen(piece, low, bits, slice(at, at + 8), 0, depth)
            read = part if read is None else jnp.where(wide == source, part, read)
        halves.append(read)
    return jnp.concatenate(halves, axis=0)


def product_reads(sources, table, which, entry, tracers):
    product = low_product(table, entry, tracers)
    high = high_part(entry, tracers)
    count = len(product) // len(sources)
    wide = jnp.broadcast_to(which, high.shape)
    read = None
    for rank, source in enumerate(sources):
        part = chosen(product[rank * count : (rank + 1) * count], high)
        read = part if read is None else jnp.where(wide == source, part, read)
    return read


def added_reads(sources, pieces, near, slot, weight, table, tracers, row, col):
    lane_terms = {k: [] for k in LANE_TERMS}
    lane_work = [(k, at) for k in LANE_TERMS for at in range(0, BLOCK, LOW)]
    products = [k for k in range(near.shape[0]) if k not in LANE_TERMS]
    total = None

    lists = [[v[k, pl.ds(row, 1), pl.ds(col, BLOCK)] for v in (near, slot, weight)] for k in range(near.shape[0])]
    for item in lists:
        inside = item[0] == sources[0]
        for source in sources[1:]:
            inside = inside | (item[0] == source)
        item[2] = jnp.where(inside, item[2], 0.0)

    for place, k in enumerate(products):
        which, entry, share = lists[k]
        term = share * product_reads(sources, table, which, entry, tracers)
        total = term if total is None else total + term
        begin, end = (len(lane_work) * p // len(products) for p in (place, place + 1))
        for lane_k, start in lane_work[begin:end]:
            which, entry, share = (v[:, start : start + LOW] for v in lists[lane_k])
            lane_terms[lane_k].append(share * lane_reads(sources, pieces, which, entry))
    for parts in lane_terms.values():
        total = total + jnp.concatenate(parts, axis=1)
    return total


def put_pieces(table, pieces):
    tracers, capacity = pieces[0].shape
    count = capacity // LOW
    for index, piece in enumerate(pieces):
        put_table(
            table, tracers, index * count, count, lambda high, piece=piece: piece[:, high * LOW : (high + 1) * LOW]
        )


def near_kernel(sources, near, slot, weight, piece, out, table):
    tracers = piece.shape[0]
    put_pieces(table, [piece])
    width = near.shape[2]
    for row in range(near.shape[1]):

        def body(step, carry, row=row):
            col = pl.multiple_of(step * BLOCK, BLOCK)
            out[:, row, pl.ds(col, BLOCK)] = added_reads(
                sources, [piece], near, slot, weight, table, tracers, row, col
            )
            return carry

        lax.fori_loop(0, width // BLOCK, body, 0)


def remap_near(source, near, slot, weight, piece):
    tracers, capacity = piece.shape
    _, rows, width = near.shape
    return pl.pallas_call(
        functools.partial(near_kernel, (source,)),
        out_shape=jax.ShapeDtypeStruct((tracers, rows, width), jnp.float32),
        scratch_shapes=[pltpu.VMEM((capacity // LOW * tracers, 2 * LOW), jnp.bfloat16)],
        compiler_params=pltpu.CompilerParams(vmem_limit_bytes=VMEM_LIMIT),
        cost_estimate=SMALL_COST,
        name="remap_near",
    )(near, slot, weight, piece)


def remap_kernel(sources, start, near, slot, weight, field, coupling, mask, partial, *rest):
    pieces, (out, table) = rest[:-2], rest[-2:]
    tracers = field.shape[0]
    put_pieces(table, pieces)
    for place in range(out.shape[1]):
        row = start[0] + place

        def body(step, carry, place=place, row=row):
            col = pl.multiple_of(step * BLOCK, BLOCK)
            at = pl.ds(col, BLOCK)
            total = added_reads(sources, pieces, near, slot, weight, table, tracers, row, col)
            total = total + partial[:, row, at]
            own = field[:, 0, row, at]
            wet = mask[pl.ds(row, 1), at].astype(jnp.float32)
            out[:, place, at] = own + coupling[:, row, at] * wet * (total - own)
            return carry

        lax.fori_loop(0, field.shape[3] // BLOCK, body, 0)


def remap(sources, start, pieces, near, slot, weight, field, coupling, mask, partial):
    tracers, capacity = pieces[0].shape
    out = (tracers, 2, field.shape[3])
    specs = [whole_spec(v.shape) for v in (near, slot, weight, coupling, mask, partial, *pieces)]
    specs.insert(3, level_spec(field))
    specs.insert(0, pl.BlockSpec(memory_space=pltpu.SMEM))
    return pl.pallas_call(
        functools.partial(remap_kernel, sources),
        grid=(1,),
        in_specs=specs,
        out_specs=whole_spec(out),
        out_shape=jax.ShapeDtypeStruct(out, jnp.float32),
        scratch_shapes=[pltpu.VMEM((len(pieces) * capacity // LOW * tracers, 2 * LOW), jnp.bfloat16)],
        compiler_params=pltpu.CompilerParams(vmem_limit_bytes=VMEM_LIMIT),
        cost_estimate=pl.CostEstimate(flops=15 * 10**9, bytes_accessed=10**6, transcendentals=0),
        name="remap",
    )(start, near, slot, weight, field, coupling, mask, partial, *pieces)


def substep(west, field, east, speed_x, speed_y):
    width = field.shape[1]
    north = pltpu.roll(field, width - 1, axis=1)
    south = pltpu.roll(field, 1, axis=1)
    return (
        (1 - 4 * diffusion) * field
        + ((diffusion - 0.5 * speed_x) * east + (diffusion + 0.5 * speed_x) * west)
        + ((diffusion - 0.5 * speed_y) * north + (diffusion + 0.5 * speed_y) * south)
    )


def transported(rows, speeds):
    for _ in range(2):
        rows = [substep(*rows[i - 1 : i + 2], *speeds[i - 1]) for i in range(1, len(rows) - 1)]
        speeds = speeds[1:-1]
    return rows


def speed_rows(velocity, before_v, after_v, level, tracers):
    levels, grid_rows = velocity.shape[1:3]
    pairs = []
    for row in range(-1, grid_rows + 1):
        pair = []
        for which in range(2):
            at = (levels - 1) * tracers + which * levels + level
            if row < 0:
                pair.append(before_v[at, 1:])
            elif row < grid_rows:
                pair.append(velocity[which, level, row : row + 1])
            else:
                pair.append(after_v[at, :1])
        pairs.append(pair)
    return pairs


def upper_kernel(first, field, before_v, after_v, velocity, *rest):
    out = rest[-1]
    level = pl.program_id(0) + (first - 1)
    tracers, _, grid_rows, _ = field.shape
    at = pl.ds(level * tracers, tracers)
    rows = [before_v[at, row] for row in range(2)]
    rows += [field[:, 0, row] for row in range(grid_rows)]
    rows += [after_v[at, row] for row in range(2)]
    speeds = speed_rows(velocity, before_v, after_v, level + 1, tracers)
    for row, value in enumerate(transported(rows, speeds)):
        out[:, 0, row] = value


def surface_kernel(start, got2, got1, velocity, before_v, after_v, own1, own2, whole, out):
    del whole
    odd = start[0] > 0
    first, last = [], []
    before, after = [], []
    for row in range(2):
        one, two = own1[:, row], own2[:, row]
        far1, far2 = got1[:, row], got2[:, row]
        first.append(jnp.where(odd, two, one))
        last.append(jnp.where(odd, one, two))
        before.append(jnp.where(odd, far2, far1))
        after.append(jnp.where(odd, far1, far2))
    speeds = speed_rows(velocity, before_v, after_v, 0, own1.shape[0])
    for row, value in enumerate(transported(before + first + last + after, speeds)):
        out[:, 0, row] = value


def whole_spec(shape):
    return pl.BlockSpec(shape, lambda *_: (0,) * len(shape))


def upper_levels(first, count, field, before_v, after_v, velocity, *whole):
    tracers, _, rows, width = field.shape
    block = (tracers, 1, rows, width)
    return pl.pallas_call(
        functools.partial(upper_kernel, first),
        grid=(count,),
        out_shape=jax.ShapeDtypeStruct(field.shape, jnp.float32),
        in_specs=[
            pl.BlockSpec(block, lambda step: (0, step + first, 0, 0)),
            whole_spec(before_v.shape),
            whole_spec(after_v.shape),
            whole_spec(velocity.shape),
        ]
        + [pl.BlockSpec(memory_space=pl.ANY)] * len(whole),
        out_specs=pl.BlockSpec(block, lambda step: (0, step + first, 0, 0)),
        input_output_aliases={4: 0} if whole else {},
        compiler_params=pltpu.CompilerParams(vmem_limit_bytes=VMEM_LIMIT),
        cost_estimate=SMALL_COST,
        name="upper_levels",
    )(field, before_v, after_v, velocity, *whole)


def surface_level(start, velocity, before_v, after_v, own1, own2, got1, got2, whole):
    tracers, _, rows, width = whole.shape
    values = (got2, got1, velocity, before_v, after_v, own1, own2)
    return pl.pallas_call(
        surface_kernel,
        grid=(1,),
        out_shape=jax.ShapeDtypeStruct(whole.shape, jnp.float32),
        in_specs=[pl.BlockSpec(memory_space=pltpu.SMEM)]
        + [whole_spec(v.shape) for v in values]
        + [pl.BlockSpec(memory_space=pl.ANY)],
        out_specs=pl.BlockSpec((tracers, 1, rows, width), lambda _: (0, 0, 0, 0)),
        input_output_aliases={len(values) + 1: 0},
        compiler_params=pltpu.CompilerParams(vmem_limit_bytes=VMEM_LIMIT),
        name="surface_level",
    )(start, *values, whole)


def per_device(
    tracer,
    velocity,
    coupling,
    sea_mask,
    send_rows,
    send_cols,
    intersection_near,
    intersection_slot,
    intersection_weight,
):
    field = tracer[0]
    speed = velocity[0]
    tracers, levels, rows, width = field.shape
    near, slot, weight = intersection_near[0], intersection_slot[0], intersection_weight[0]
    others = (0, 2, 3)
    before_v, after_v = edges(field, speed)
    before_v, lists = lax.optimization_barrier((before_v, (send_rows[0, 0], send_cols[0, 0])))
    packed = pack(field, *lists)
    before_v = moved(before_v, 1, False)
    pieces = [moved(packed[j], 1 - j, True) for j in range(len(packed))]
    after_v = moved(after_v, -1, False)
    partial = remap_near(1, near, slot, weight, pieces[1])
    pieces, before_v = lax.optimization_barrier(([pieces[j] for j in others], before_v))
    shared = (near, slot, weight, field, coupling[0], sea_mask[0], partial)
    odd = lax.axis_index("tile") & 1
    start1, start2 = (2 * odd).reshape(1), (2 - 2 * odd).reshape(1)
    own1 = remap(others, start1, pieces, *shared)
    got1 = swapped(own1, 1)
    pieces, own1 = lax.optimization_barrier((pieces, own1))
    own2 = remap(others, start2, pieces, *shared)
    got2 = swapped(own2, -1)
    whole = upper_levels(1, levels - 2, field, before_v, after_v, speed)
    whole, got1 = lax.optimization_barrier((whole, got1))
    whole = upper_levels(levels - 1, 1, field, before_v, after_v, speed, whole)
    return surface_level(start1, speed, before_v, after_v, own1, own2, got1, got2, whole)[None]


def solution(mesh):
    in_specs = (
        P("comp", None, None, "tile", None),
        P("comp", None, None, "tile", None),
        P("comp", None, "tile", None),
        P("comp", "tile", None),
        P("comp", "tile", None, None),
        P("comp", "tile", None, None),
        P("comp", None, "tile", None),
        P("comp", None, "tile", None),
        P("comp", None, "tile", None),
    )
    out_specs = P("comp", None, None, "tile", None)
    return jax.shard_map(
        per_device, mesh=mesh, in_specs=in_specs, out_specs=out_specs, check_vma=False
    )
```

```python
import functools

import jax
import jax.numpy as jnp
from jax import lax
from jax.experimental import pallas as pl
from jax.experimental.pallas import tpu as pltpu
from jax.sharding import PartitionSpec as P

diffusion = 0.12
LOW = 128
BLOCK = 1024
LANE_TERMS = (0, 1)
PACK_BLOCK = 512
VMEM_LIMIT = 48 * 2**20
FULL_VMEM = 60 * 2**20
SMALL_COST = pl.CostEstimate(flops=10**6, bytes_accessed=10**5, transcendentals=0)


def moved(value, steps, swap):
    tiles = lax.axis_size("tile")
    pairs = []
    for comp in range(lax.axis_size("comp")):
        for tile in range(tiles):
            target = (comp ^ 1 if swap else comp) * tiles + (tile + steps) % tiles
            pairs.append((comp * tiles + tile, target))
    return lax.ppermute(value, ("comp", "tile"), pairs)


def swapped(value, odd_step):
    tiles = lax.axis_size("tile")
    pairs = [(tile, (tile + (odd_step if tile % 2 else -odd_step)) % tiles) for tile in range(tiles)]
    return lax.ppermute(value, "tile", pairs)


def put_table(table, tracers, first, count, part):
    for high in range(count):
        value = part(high)
        leading = value.astype(jnp.bfloat16)
        rest = (value - leading.astype(jnp.float32)).astype(jnp.bfloat16)
        row = (first + high) * tracers
        table[row : row + tracers, :] = jnp.concatenate([leading, rest], axis=1)


def one_hot(low):
    width = low.shape[1]
    position = lax.broadcasted_iota(jnp.int32, (LOW, width), 0).astype(jnp.float32).astype(jnp.bfloat16)
    wanted = jnp.broadcast_to(low.astype(jnp.float32), (16, width)).astype(jnp.bfloat16)
    wanted = jnp.concatenate([wanted] * (LOW // 16), axis=0)
    return jnp.where(position == wanted, jnp.bfloat16(1), jnp.bfloat16(0))


def chosen(values, high):
    bit = 0
    while len(values) > 1:
        odd = ((high >> bit) & 1) == 1
        values = [jnp.where(odd, values[i + 1], values[i]) for i in range(0, len(values), 2)]
        bit += 1
    return values[0]


def low_product(table, entry, tracers):
    hot = one_hot(entry & (LOW - 1))
    hot = jnp.concatenate([hot, hot], axis=0)
    product = jnp.dot(table[...], hot, preferred_element_type=jnp.float32)
    return [product[at : at + tracers] for at in range(0, table.shape[0], tracers)]


def high_part(entry, tracers):
    return jnp.broadcast_to(entry // LOW, (tracers, entry.shape[1]))


def started(pairs, sems):
    copies = [pltpu.make_async_copy(source, target, sems.at[i]) for i, (source, target) in enumerate(pairs)]
    for copy in copies:
        copy.start()
    return copies


def edges_kernel(field, speed, before_v, after_v, upper, moving, sems):
    tracers, levels, grid_rows, _ = field.shape
    for copy in started(((speed, moving), (field.at[:, pl.ds(1, levels - 1)], upper)), sems):
        copy.wait()
    for which in range(2):
        for level in range(levels):
            at = (levels - 1) * tracers + level
            after_v[at, which : which + 1] = moving[which, level, :1]
            before_v[at, which : which + 1] = moving[which, level, grid_rows - 1 :]
    for level in range(levels - 1):
        at = slice(level * tracers, (level + 1) * tracers)
        after_v[at] = upper[:, level, :2]
        before_v[at] = upper[:, level, grid_rows - 2 :]


def edges(field, speed):
    tracers, levels, grid_rows, width = field.shape
    edge = jax.ShapeDtypeStruct(((levels - 1) * tracers + levels, 2, width), jnp.float32)
    return pl.pallas_call(
        edges_kernel,
        in_specs=[pl.BlockSpec(memory_space=pltpu.HBM)] * 2,
        out_shape=[edge, edge],
        scratch_shapes=[
            pltpu.VMEM((tracers, levels - 1, grid_rows, width), jnp.float32),
            pltpu.VMEM(speed.shape, jnp.float32),
            pltpu.SemaphoreType.DMA((2,)),
        ],
        compiler_params=pltpu.CompilerParams(vmem_limit_bytes=FULL_VMEM),
        cost_estimate=SMALL_COST,
        name="edges",
    )(field, speed)


def pack_kernel(field, rows, cols, *rest):
    outs, table = rest[:-1], rest[-1]
    tracers, _, grid_rows, width = field.shape
    per_row = width // LOW

    def part(high):
        low = high % per_row * LOW
        return field[:, 0, high // per_row, low : low + LOW]

    put_table(table, tracers, 0, grid_rows * per_row, part)
    for near in range(rows.shape[0]):
        for start in range(0, rows.shape[1], PACK_BLOCK):
            at = slice(start, start + PACK_BLOCK)
            entry = rows[near : near + 1, at] * width + cols[near : near + 1, at]
            product = low_product(table, entry, tracers)
            outs[near][:, at] = chosen(product, high_part(entry, tracers))


def level_spec(field):
    tracers, _, rows, width = field.shape
    return pl.BlockSpec((tracers, 1, rows, width), lambda *_: (0, 0, 0, 0))


def pack(field, rows, cols):
    tracers, _, grid_rows, width = field.shape
    neighbours, capacity = rows.shape
    piece = jax.ShapeDtypeStruct((tracers, capacity), jnp.float32)
    return pl.pallas_call(
        pack_kernel,
        grid=(1,),
        in_specs=[level_spec(field), whole_spec(rows.shape), whole_spec(cols.shape)],
        out_specs=[whole_spec(piece.shape)] * neighbours,
        out_shape=[piece] * neighbours,
        scratch_shapes=[pltpu.VMEM((grid_rows * width // LOW * tracers, 2 * LOW), jnp.bfloat16)],
        compiler_params=pltpu.CompilerParams(vmem_limit_bytes=VMEM_LIMIT),
        cost_estimate=SMALL_COST,
        name="pack",
    )(field, rows, cols)


def lane_chosen(piece, low, bits, rows, first, level):
    if level == 0:
        part = piece[rows, first * LOW : (first + 1) * LOW]
        return jnp.take_along_axis(part, low, axis=1, mode="promise_in_bounds")
    half = 1 << (level - 1)
    even = lane_chosen(piece, low, bits, rows, first, level - 1)
    odd = lane_chosen(piece, low, bits, rows, first + half, level - 1)
    return jnp.where(bits[level - 1], odd, even)


def lane_reads(sources, pieces, which, entry):
    tracers, capacity = pieces[0].shape
    low = jnp.broadcast_to(entry & (LOW - 1), (8, LOW))
    high = jnp.broadcast_to(entry // LOW, (8, LOW))
    wide = jnp.broadcast_to(which, (8, LOW))
    depth = (capacity // LOW).bit_length() - 1
    bits = [((high >> bit) & 1) == 1 for bit in range(depth)]
    halves = []
    for at in range(0, tracers, 8):
        read = None
        for source, piece in zip(sources, pieces):
            part = lane_chosen(piece, low, bits, slice(at, at + 8), 0, depth)
            read = part if read is None else jnp.where(wide == source, part, read)
        halves.append(read)
    return jnp.concatenate(halves, axis=0)


def product_reads(sources, table, which, entry, tracers):
    product = low_product(table, entry, tracers)
    high = high_part(entry, tracers)
    count = len(product) // len(sources)
    wide = jnp.broadcast_to(which, high.shape)
    read = None
    for rank, source in enumerate(sources):
        part = chosen(product[rank * count : (rank + 1) * count], high)
        read = part if read is None else jnp.where(wide == source, part, read)
    return read


def added_reads(sources, pieces, near, slot, weight, table, tracers, row, col):
    lane_terms = {k: [] for k in LANE_TERMS}
    lane_work = [(k, at) for k in LANE_TERMS for at in range(0, BLOCK, LOW)]
    products = [k for k in range(near.shape[0]) if k not in LANE_TERMS]
    total = None

    lists = [[v[k, pl.ds(row, 1), pl.ds(col, BLOCK)] for v in (near, slot, weight)] for k in range(near.shape[0])]
    for item in lists:
        inside = item[0] == sources[0]
        for source in sources[1:]:
            inside = inside | (item[0] == source)
        item[2] = jnp.where(inside, item[2], 0.0)

    for place, k in enumerate(products):
        which, entry, share = lists[k]
        term = share * product_reads(sources, table, which, entry, tracers)
        total = term if total is None else total + term
        begin, end = (len(lane_work) * p // len(products) for p in (place, place + 1))
        for lane_k, start in lane_work[begin:end]:
            which, entry, share = (v[:, start : start + LOW] for v in lists[lane_k])
            lane_terms[lane_k].append(share * lane_reads(sources, pieces, which, entry))
    for parts in lane_terms.values():
        total = total + jnp.concatenate(parts, axis=1)
    return total


def put_pieces(table, pieces):
    tracers, capacity = pieces[0].shape
    count = capacity // LOW
    for index, piece in enumerate(pieces):
        put_table(
            table, tracers, index * count, count, lambda high, piece=piece: piece[:, high * LOW : (high + 1) * LOW]
        )


def near_kernel(sources, near, slot, weight, piece, out, table):
    tracers = piece.shape[0]
    put_pieces(table, [piece])
    width = near.shape[2]
    for row in range(near.shape[1]):

        def body(step, carry, row=row):
            col = pl.multiple_of(step * BLOCK, BLOCK)
            out[:, row, pl.ds(col, BLOCK)] = added_reads(
                sources, [piece], near, slot, weight, table, tracers, row, col
            )
            return carry

        lax.fori_loop(0, width // BLOCK, body, 0)


def remap_near(source, near, slot, weight, piece):
    tracers, capacity = piece.shape
    _, rows, width = near.shape
    return pl.pallas_call(
        functools.partial(near_kernel, (source,)),
        out_shape=jax.ShapeDtypeStruct((tracers, rows, width), jnp.float32),
        scratch_shapes=[pltpu.VMEM((capacity // LOW * tracers, 2 * LOW), jnp.bfloat16)],
        compiler_params=pltpu.CompilerParams(vmem_limit_bytes=VMEM_LIMIT),
        cost_estimate=SMALL_COST,
        name="remap_near",
    )(near, slot, weight, piece)


def remap_kernel(sources, start, near, slot, weight, field, coupling, mask, partial, *rest):
    pieces, (out, table) = rest[:-2], rest[-2:]
    tracers = field.shape[0]
    put_pieces(table, pieces)
    for place in range(out.shape[1]):
        row = start[0] + place

        def body(step, carry, place=place, row=row):
            col = pl.multiple_of(step * BLOCK, BLOCK)
            at = pl.ds(col, BLOCK)
            total = added_reads(sources, pieces, near, slot, weight, table, tracers, row, col)
            total = total + partial[:, row, at]
            own = field[:, 0, row, at]
            wet = mask[pl.ds(row, 1), at].astype(jnp.float32)
            out[:, place, at] = own + coupling[:, row, at] * wet * (total - own)
            return carry

        lax.fori_loop(0, field.shape[3] // BLOCK, body, 0)


def remap(sources, start, pieces, near, slot, weight, field, coupling, mask, partial):
    tracers, capacity = pieces[0].shape
    out = (tracers, 2, field.shape[3])
    specs = [whole_spec(v.shape) for v in (near, slot, weight, coupling, mask, partial, *pieces)]
    specs.insert(3, level_spec(field))
    specs.insert(0, pl.BlockSpec(memory_space=pltpu.SMEM))
    return pl.pallas_call(
        functools.partial(remap_kernel, sources),
        grid=(1,),
        in_specs=specs,
        out_specs=whole_spec(out),
        out_shape=jax.ShapeDtypeStruct(out, jnp.float32),
        scratch_shapes=[pltpu.VMEM((len(pieces) * capacity // LOW * tracers, 2 * LOW), jnp.bfloat16)],
        compiler_params=pltpu.CompilerParams(vmem_limit_bytes=VMEM_LIMIT),
        cost_estimate=pl.CostEstimate(flops=15 * 10**9, bytes_accessed=10**6, transcendentals=0),
        name="remap",
    )(start, near, slot, weight, field, coupling, mask, partial, *pieces)


def substep(west, field, east, speed_x, speed_y):
    width = field.shape[1]
    north = pltpu.roll(field, width - 1, axis=1)
    south = pltpu.roll(field, 1, axis=1)
    return (
        (1 - 4 * diffusion) * field
        + ((diffusion - 0.5 * speed_x) * east + (diffusion + 0.5 * speed_x) * west)
        + ((diffusion - 0.5 * speed_y) * north + (diffusion + 0.5 * speed_y) * south)
    )


def transported(rows, speeds):
    for _ in range(2):
        rows = [substep(*rows[i - 1 : i + 2], *speeds[i - 1]) for i in range(1, len(rows) - 1)]
        speeds = speeds[1:-1]
    return rows


def speed_rows(velocity, before_v, after_v, level, tracers):
    levels, grid_rows = velocity.shape[1:3]
    pairs = []
    for row in range(-1, grid_rows + 1):
        pair = []
        for which in range(2):
            at = (levels - 1) * tracers + level
            if row < 0:
                pair.append(before_v[at, which : which + 1])
            elif row < grid_rows:
                pair.append(velocity[which, level, row : row + 1])
            else:
                pair.append(after_v[at, which : which + 1])
        pairs.append(pair)
    return pairs


def upper_kernel(first, field, before_v, after_v, velocity, *rest):
    out = rest[-1]
    level = pl.program_id(0) + (first - 1)
    tracers, _, grid_rows, _ = field.shape
    at = pl.ds(level * tracers, tracers)
    rows = [before_v[at, row] for row in range(2)]
    rows += [field[:, 0, row] for row in range(grid_rows)]
    rows += [after_v[at, row] for row in range(2)]
    speeds = speed_rows(velocity, before_v, after_v, level + 1, tracers)
    for row, value in enumerate(transported(rows, speeds)):
        out[:, 0, row] = value


def surface_kernel(start, got2, got1, velocity, before_v, after_v, own1, own2, whole, out):
    del whole
    odd = start[0] > 0
    first, last = [], []
    before, after = [], []
    for row in range(2):
        one, two = own1[:, row], own2[:, row]
        far1, far2 = got1[:, row], got2[:, row]
        first.append(jnp.where(odd, two, one))
        last.append(jnp.where(odd, one, two))
        before.append(jnp.where(odd, far2, far1))
        after.append(jnp.where(odd, far1, far2))
    speeds = speed_rows(velocity, before_v, after_v, 0, own1.shape[0])
    for row, value in enumerate(transported(before + first + last + after, speeds)):
        out[:, 0, row] = value


def whole_spec(shape):
    return pl.BlockSpec(shape, lambda *_: (0,) * len(shape))


def upper_levels(first, count, field, before_v, after_v, velocity, *whole):
    tracers, _, rows, width = field.shape
    block = (tracers, 1, rows, width)
    return pl.pallas_call(
        functools.partial(upper_kernel, first),
        grid=(count,),
        out_shape=jax.ShapeDtypeStruct(field.shape, jnp.float32),
        in_specs=[
            pl.BlockSpec(block, lambda step: (0, step + first, 0, 0)),
            whole_spec(before_v.shape),
            whole_spec(after_v.shape),
            whole_spec(velocity.shape),
        ]
        + [pl.BlockSpec(memory_space=pl.ANY)] * len(whole),
        out_specs=pl.BlockSpec(block, lambda step: (0, step + first, 0, 0)),
        input_output_aliases={4: 0} if whole else {},
        compiler_params=pltpu.CompilerParams(vmem_limit_bytes=VMEM_LIMIT),
        cost_estimate=SMALL_COST,
        name="upper_levels",
    )(field, before_v, after_v, velocity, *whole)


def surface_level(start, velocity, before_v, after_v, own1, own2, got1, got2, whole):
    tracers, _, rows, width = whole.shape
    values = (got2, got1, velocity, before_v, after_v, own1, own2)
    return pl.pallas_call(
        surface_kernel,
        grid=(1,),
        out_shape=jax.ShapeDtypeStruct(whole.shape, jnp.float32),
        in_specs=[pl.BlockSpec(memory_space=pltpu.SMEM)]
        + [whole_spec(v.shape) for v in values]
        + [pl.BlockSpec(memory_space=pl.ANY)],
        out_specs=pl.BlockSpec((tracers, 1, rows, width), lambda _: (0, 0, 0, 0)),
        input_output_aliases={len(values) + 1: 0},
        compiler_params=pltpu.CompilerParams(vmem_limit_bytes=VMEM_LIMIT),
        name="surface_level",
    )(start, *values, whole)


def per_device(
    tracer,
    velocity,
    coupling,
    sea_mask,
    send_rows,
    send_cols,
    intersection_near,
    intersection_slot,
    intersection_weight,
):
    field = tracer[0]
    speed = velocity[0]
    tracers, levels, rows, width = field.shape
    near, slot, weight = intersection_near[0], intersection_slot[0], intersection_weight[0]
    others = (0, 2, 3)
    before_v, after_v = edges(field, speed)
    before_v, lists = lax.optimization_barrier((before_v, (send_rows[0, 0], send_cols[0, 0])))
    packed = pack(field, *lists)
    before_v = moved(before_v, 1, False)
    pieces = [moved(packed[j], 1 - j, True) for j in range(len(packed))]
    after_v = moved(after_v, -1, False)
    partial = remap_near(1, near, slot, weight, pieces[1])
    pieces, before_v = lax.optimization_barrier(([pieces[j] for j in others], before_v))
    shared = (near, slot, weight, field, coupling[0], sea_mask[0], partial)
    odd = lax.axis_index("tile") & 1
    start1, start2 = (2 * odd).reshape(1), (2 - 2 * odd).reshape(1)
    own1 = remap(others, start1, pieces, *shared)
    got1 = swapped(own1, 1)
    pieces, own1 = lax.optimization_barrier((pieces, own1))
    own2 = remap(others, start2, pieces, *shared)
    got2 = swapped(own2, -1)
    whole = upper_levels(1, levels - 2, field, before_v, after_v, speed)
    whole, got1 = lax.optimization_barrier((whole, got1))
    whole = upper_levels(levels - 1, 1, field, before_v, after_v, speed, whole)
    return surface_level(start1, speed, before_v, after_v, own1, own2, got1, got2, whole)[None]


def solution(mesh):
    in_specs = (
        P("comp", None, None, "tile", None),
        P("comp", None, None, "tile", None),
        P("comp", None, "tile", None),
        P("comp", "tile", None),
        P("comp", "tile", None, None),
        P("comp", "tile", None, None),
        P("comp", None, "tile", None),
        P("comp", None, "tile", None),
        P("comp", None, "tile", None),
    )
    out_specs = P("comp", None, None, "tile", None)
    return jax.shard_map(
        per_device, mesh=mesh, in_specs=in_specs, out_specs=out_specs, check_vma=False
    )
```
